512 devices in a mesh: dp: 512 (over x, z, y, core).
Axes of the slice: x: 4, y: 4, z: 16, core: 2. Of those that a mesh axis runs over, the one named last changes fastest.
Arguments:
- embeddings: float32 [425984, 1024], P('dp'), as said below
- start_basis: float32 [425984, 256], P('dp'), may hold values from -6 to 6
Outputs:
- basis: float32 [425984, 256], P('dp')
The draws below stay inside these ranges and needn't reach their ends.
Inputs may be any that keep to these rules, and one draw needn't show every extreme that they name: `embeddings`: rows and columns of the slab have differing scales; entries are independent within them, apart from a small common offset per column.
All inputs are finite; a program needn't handle non-finite values.
Results may differ from the reference program's by a relative error of at most 0.00015.
Values sent between devices are 32-bit elements; how exact they have to be, the bound alone decides.
A program may use at most 64 MiB of HBM per device.

```python
import jax
import jax.numpy as jnp
from jax import lax

D = 1024
K = 256
ROWS = 425984


def draw_embeddings(key, part):
    key = jax.random.fold_in(key, 7)
    key_rows, key_cols, key_vals = jax.random.split(key, 3)
    low = jnp.log(jnp.float32(0.3))
    high = jnp.log(jnp.float32(3.0))
    row_scale = jnp.exp(jax.random.uniform(key_rows, (ROWS, 1), jnp.float32, low, high))
    col_scale = jnp.exp(jax.random.uniform(key_cols, (1, D), jnp.float32, low, high))
    values = jax.random.normal(key_vals, (ROWS, D), jnp.float32)
    return values * row_scale * col_scale


def shard_levels(own_key, dims, cuts, least, largest):
    level = 1.0
    for position, parts in cuts:
        draws = jax.random.uniform(jax.random.fold_in(jax.random.fold_in(own_key, 6), position), (parts,), jnp.float32, least / len(cuts), largest / len(cuts))
        level = level * jnp.repeat(jnp.exp(draws), dims[position] // parts).reshape((-1,) + (1,) * (len(dims) - 1 - position))
    return level


def bell_draw(stream_key, dims, width, most, cuts=(), held_as=jnp.bfloat16):
    result = jax.random.normal(stream_key, dims, jnp.float32) * width
    if len(cuts) > 0:
        result = shard_levels(stream_key, dims, cuts, -0.22, 0.18) * result
    return jnp.clip(result, min=-most, max=most).astype(held_as)


def setup_inputs(seed: int = 0) -> dict:
    key_list = jax.random.split(jax.random.key(seed), 3)
    embeddings = draw_embeddings(jax.random.fold_in(key_list[2], 71), 0)
    start_basis = bell_draw(key_list[1], (ROWS, K), 1.0, 6.0, ((0, 512),), jnp.float32)
    return dict(embeddings=embeddings, start_basis=start_basis)


def reference(embeddings, start_basis):
    sketch = lax.dot_general(embeddings.astype(jnp.float32), start_basis.astype(jnp.float32), (((0,), (0,)), ((), ())), precision=lax.Precision.HIGHEST, preferred_element_type=jnp.float32)
    image = jnp.dot(embeddings.astype(jnp.float32), sketch.astype(jnp.float32), precision=lax.Precision.HIGHEST, preferred_element_type=jnp.float32)
    gram = lax.dot_general(image.astype(jnp.float32), image.astype(jnp.float32), (((0,), (0,)), ((), ())), precision=lax.Precision.HIGHEST, preferred_element_type=jnp.float32)
    lower = jnp.linalg.cholesky(gram)
    solved = lax.linalg.triangular_solve(lower, image, left_side=False, lower=True, transpose_a=True)
    return solved * jnp.sqrt(jnp.float32(ROWS))
```

```python
import functools

import jax
import jax.numpy as jnp
from jax import lax
from jax.experimental import pallas as pl
from jax.experimental.pallas import tpu as pltpu
from jax.sharding import PartitionSpec as P

F32, BF16 = jnp.float32, jnp.bfloat16
NX, NZ, NY, NC = 4, 16, 4, 2
PLANE = NX * NY
D, K = 1024, 256
PARTS = 4
WIDE = D // PARTS
TILES = D // 128

PLANE_STEPS = sorted(
    [(dx, dy) for dx in range(NX) for dy in range(NY) if (dx, dy) != (0, 0)],
    key=lambda s: -(min(s[0], NX - s[0]) + min(s[1], NY - s[1])),
)
PLANE_CORE_STEPS = [(dx, dy, dc) for dx, dy in PLANE_STEPS for dc in range(NC)] + [(0, 0, 1)]
Z_STEPS = sorted(range(1, NZ), key=lambda d: -min(d, NZ - d))

NT = (((1,), (1,)), ((), ()))
NN = (((1,), (0,)), ((), ()))
TN = (((0,), (0,)), ((), ()))


def mm(a, b, dims):
    return lax.dot_general(a, b, dims, preferred_element_type=F32)


def split2(value):
    high = value.astype(BF16)
    return high, (value - high.astype(F32)).astype(BF16)


def split3(value):
    high = value.astype(BF16)
    rest = value - high.astype(F32)
    middle = rest.astype(BF16)
    return high, middle, (rest - middle.astype(F32)).astype(BF16)


def device(x, z, y, c):
    return ((x * NZ + z) * NY + y) * NC + c


def remote(src, dst, send, recv, target):
    return pltpu.make_async_remote_copy(
        src_ref=src,
        dst_ref=dst,
        send_sem=send,
        recv_sem=recv,
        device_id={"dp": target},
        device_id_type=pl.DeviceIdType.MESH,
    )


def gather_kernel(
    emb_hbm, start_hbm, image_hbm, gram_ref,
    emb, emb_hi, emb_lo, start, part, core_in, plane_in, tiles, z_in, sketch,
    image, gram_part, gram_in, gram_z, gram_all_,
    load_sem, core_s, core_r, xs, xr, zs, zr, ags, agr, bs, br, fs, fr, gs, gr, hs, hr, ks, kr, out_sem,
):
    me = lax.axis_index("dp")
    x, z, y, c = me // (NZ * NY * NC), (me // (NY * NC)) % NZ, (me // NC) % NY, me % NC
    p = x * NY + y
    plane = [((x + dx) % NX, (y + dy) % NY) for dx, dy in PLANE_STEPS]
    plane_core = [((x + dx) % NX, (y + dy) % NY, (c + dc) % NC) for dx, dy, dc in PLANE_CORE_STEPS]
    sibling = device(x, z, y, 1 - c)

    loads = [pltpu.make_async_copy(start_hbm, start, load_sem.at[PARTS])]
    loads += [
        pltpu.make_async_copy(emb_hbm.at[:, pl.ds(i * WIDE, WIDE)], emb.at[i], load_sem.at[i])
        for i in range(PARTS)
    ]
    for copy in loads:
        copy.start()

    barrier = pltpu.get_barrier_semaphore()
    for zs_ in Z_STEPS:
        pl.semaphore_signal(barrier, inc=1, device_id={"dp": device(x, (z + zs_) % NZ, y, c)}, device_id_type=pl.DeviceIdType.MESH)
    for qx, qy, qc in plane_core:
        pl.semaphore_signal(barrier, inc=1, device_id={"dp": device(qx, z, qy, qc)}, device_id_type=pl.DeviceIdType.MESH)

    loads[0].wait()
    start_hi, start_lo = split2(start[...].T)

    def core_copy(i):
        return remote(
            part.at[pl.ds((1 - c) * PLANE, PLANE), :, pl.ds(i * WIDE, WIDE)],
            core_in.at[:, :, pl.ds(i * WIDE, WIDE)],
            core_s.at[i], core_r.at[i], sibling,
        )

    for i in range(PARTS):
        loads[1 + i].wait()
        hi, lo = split2(emb[i])
        emb_hi[i] = hi
        emb_lo[i] = lo
        total = mm(start_hi, hi, NN) + (mm(start_hi, lo, NN) + mm(start_lo, hi, NN))
        part[:, :, i * WIDE:(i + 1) * WIDE] = total.reshape(NC * PLANE, 8, WIDE)
        if i == 0:
            pl.semaphore_wait(barrier, len(Z_STEPS) + len(plane_core))
        core_copy(i).start()
    own = pl.ds(c * PLANE, PLANE)
    for i in range(PARTS):
        core_copy(i).wait_recv()
        cols = slice(i * WIDE, (i + 1) * WIDE)
        part[own, :, cols] = part[own, :, cols] + core_in[:, :, cols]

    def plane_copy(o):
        qx, qy = plane[o]
        return remote(part.at[c * PLANE + qx * NY + qy], plane_in.at[o], xs.at[o], xr.at[o], device(qx, z, qy, c))

    for o in range(PLANE - 1):
        plane_copy(o).start()
    for o in range(PLANE - 1):
        plane_copy(o).wait_recv()
    total = part[c * PLANE + p]
    for o in range(PLANE - 1):
        total = total + plane_in[o]
    for t in range(TILES):
        tiles[t] = total[:, t * 128:(t + 1) * 128]

    owner = z % NC == c
    mine = z // NC
    slot = c * PLANE + p

    def z_copy(t):
        target = NC * t + c
        step = (target - z + NZ) % NZ
        return remote(tiles.at[t], z_in.at[step], zs.at[t], zr.at[step], device(x, target, y, c))

    for t in range(TILES):
        @pl.when(NC * t + c != z)
        def _(t=t):
            z_copy(t).start()

    def tile_of(t):
        return sketch.at[slot, :, pl.ds(pl.multiple_of(t * 128, 128), 128)]

    def z_out(step):
        return remote(tile_of(mine), tile_of(mine), ags.at[step], agr.at[mine], device(x, (z + step) % NZ, y, c))

    @pl.when(owner)
    def _():
        for step in Z_STEPS:
            remote(tiles.at[0], z_in.at[step], zs.at[0], zr.at[step], me).wait_recv()
        total = tiles[mine]
        for step in range(1, NZ):
            total = total + z_in[step]
        sketch[slot, :, pl.ds(pl.multiple_of(mine * 128, 128), 128)] = total
        for step in Z_STEPS:
            z_out(step).start()

    for t in range(TILES):
        @pl.when(NC * t + c != z)
        def _(t=t):
            remote(tile_of(t), tile_of(t), ags.at[0], agr.at[t], me).wait_recv()

    def plane_out(o):
        qx, qy = plane[o]
        return remote(sketch.at[slot], sketch.at[slot], bs.at[o], br.at[o], device(qx, z, qy, c))

    def source(o):
        dx, dy = PLANE_STEPS[o]
        return ((x - dx + NX) % NX) * NY + (y - dy + NY) % NY

    def forward(o):
        index = c * PLANE + (p if o == PLANE - 1 else source(o))
        return remote(sketch.at[index], sketch.at[index], fs.at[o], fr.at[o], sibling)

    for o in range(PLANE - 1):
        plane_out(o).start()
    forward(PLANE - 1).start()
    for o in reversed(range(PLANE - 1)):
        index = c * PLANE + source(o)
        remote(sketch.at[index], sketch.at[index], bs.at[o], br.at[o], me).wait_recv()
        forward(o).start()
    for o in range(PLANE):
        index = (1 - c) * PLANE + (p if o == PLANE - 1 else source(o))
        remote(sketch.at[index], sketch.at[index], fs.at[o], fr.at[o], me).wait_recv()

    total = None
    for i in range(PARTS):
        hi, lo = split2(sketch[:, :, i * WIDE:(i + 1) * WIDE].reshape(K, WIDE))
        term = mm(emb_hi[i], hi, NT) + (mm(emb_hi[i], lo, NT) + mm(emb_lo[i], hi, NT))
        total = term if total is None else total + term
    image[...] = total
    image_copy = pltpu.make_async_copy(image, image_hbm, out_sem)
    image_copy.start()
    turned = total.T
    ah, am, al = split3(turned)
    bh, bm, bl = split3(total)
    gram = mm(ah, bh, NN) + (mm(ah, bm, NN) + mm(am, bh, NN)) + (mm(am, bm, NN) + (mm(ah, bl, NN) + mm(al, bh, NN)))
    row = lax.broadcasted_iota(jnp.int32, (128, 128), 0)
    col = lax.broadcasted_iota(jnp.int32, (128, 128), 1)
    corner = gram[128:, 128:]
    diag = jnp.sum(jnp.where(row == col, corner, 0.0), axis=0, keepdims=True)
    gram_part[0:16, 0:8] = jnp.where(row >= col, gram[:128, :128], corner).reshape(16, 8, 128)
    gram_part[16:32, 0:8] = gram[:128, 128:].reshape(16, 8, 128)
    gram_part[:, 8:9] = jnp.broadcast_to(diag[None], (32, 1, 128))

    def gram_copy(o):
        qx, qy, qc = plane_core[o]
        return remote(gram_part.at[(qx * NY + qy) * NC + qc], gram_in.at[o], gs.at[o], gr.at[o], device(qx, z, qy, qc))

    for o in range(len(plane_core)):
        gram_copy(o).start()
    for o in range(len(plane_core)):
        gram_copy(o).wait_recv()
    block = p * NC + c
    total = gram_part[block]
    for o in range(len(plane_core)):
        total = total + gram_in[o]
    gram_z[z] = total

    def gram_z_copy(step):
        return remote(gram_z.at[z], gram_z.at[z], hs.at[step], hr.at[step], device(x, (z + step) % NZ, y, c))

    for step in Z_STEPS:
        gram_z_copy(step).start()
    for step in reversed(Z_STEPS):
        src = (z - step + NZ) % NZ
        remote(gram_z.at[src], gram_z.at[src], hs.at[step], hr.at[step], me).wait_recv()
    total = gram_z[0]
    for i in range(1, NZ):
        total = total + gram_z[i]
    gram_all_[block] = total

    def gram_out(o):
        qx, qy, qc = plane_core[o]
        return remote(gram_all_.at[block], gram_all_.at[block], ks.at[o], kr.at[o], device(qx, z, qy, qc))

    for o in range(len(plane_core)):
        gram_out(o).start()
    for o in reversed(range(len(plane_core))):
        dx, dy, dc = PLANE_CORE_STEPS[o]
        index = (((x - dx + NX) % NX) * NY + (y - dy + NY) % NY) * NC + (c + dc) % NC
        remote(gram_all_.at[index], gram_all_.at[index], ks.at[o], kr.at[o], me).wait_recv()
    gram_ref[...] = gram_all_[...]

    image_copy.wait()
    for i in range(PARTS):
        core_copy(i).wait_send()
    for o in range(PLANE - 1):
        plane_copy(o).wait_send()
        plane_out(o).wait_send()
    for t in range(TILES):
        @pl.when(NC * t + c != z)
        def _(t=t):
            z_copy(t).wait_send()

    @pl.when(owner)
    def _():
        for step in Z_STEPS:
            z_out(step).wait_send()
    for o in range(PLANE):
        forward(o).wait_send()
    for o in range(len(plane_core)):
        gram_copy(o).wait_send()
        gram_out(o).wait_send()
    for step in Z_STEPS:
        gram_z_copy(step).wait_send()


def sums(embeddings, start_basis):
    rows = embeddings.shape[0]
    dma = lambda n: pltpu.SemaphoreType.DMA((n,))
    vmem = pltpu.VMEM
    return pl.pallas_call(
        gather_kernel,
        out_shape=(
            jax.ShapeDtypeStruct((rows, K), F32),
            jax.ShapeDtypeStruct((32, 9, 128), F32),
        ),
        in_specs=[pl.BlockSpec(memory_space=pl.ANY)] * 2,
        out_specs=(pl.BlockSpec(memory_space=pl.ANY), pl.BlockSpec(memory_space=pltpu.VMEM)),
        scratch_shapes=[
            vmem((PARTS, rows, WIDE), F32),
            vmem((PARTS, rows, WIDE), BF16),
            vmem((PARTS, rows, WIDE), BF16),
            vmem((rows, K), F32),
            vmem((NC * PLANE, 8, D), F32),
            vmem((PLANE, 8, D), F32),
            vmem((PLANE - 1, 8, D), F32),
            vmem((TILES, 8, 128), F32),
            vmem((NZ, 8, 128), F32),
            vmem((NC * PLANE, 8, D), F32),
            vmem((rows, K), F32),
            vmem((32, 9, 128), F32),
            vmem((31, 9, 128), F32),
            vmem((NZ, 9, 128), F32),
            vmem((32, 9, 128), F32),
            dma(PARTS + 1),
            dma(PARTS), dma(PARTS),
            dma(PLANE), dma(PLANE),
            dma(TILES), dma(NZ),
            dma(NZ), dma(TILES),
            dma(PLANE), dma(PLANE),
            dma(PLANE), dma(PLANE),
            dma(32), dma(32),
            dma(NZ), dma(NZ),
            dma(32), dma(32),
            pltpu.SemaphoreType.DMA,
        ],
        compiler_params=pltpu.CompilerParams(
            collective_id=0, has_side_effects=True, vmem_limit_bytes=48 << 20
        ),
        name="sums",
    )(embeddings, start_basis)


def factor_block(cols, strips, size):
    rows = lax.broadcasted_iota(jnp.int32, (size, 128), 0)
    scale = jnp.zeros((size, 128), F32)
    for j in range(0, size, 2):
        cj, cn = cols[j], cols[j + 1]
        a, b, d = cj[j:j + 1], cj[j + 1:j + 2], cn[j + 1:j + 2]
        q = 1.0 / (a * d - b * b)
        aq, bq, dq = a * q, b * q, d * q
        u = cj * dq - cn * bq
        v = cn * aq - cj * bq
        for k in range(j + 2, size):
            lo = (k // 8) * 8
            new = cols[k][lo:] - (u[lo:] * cj[k:k + 1] + v[lo:] * cn[k:k + 1])
            cols[k] = jnp.concatenate([cols[k][:lo], new], 0) if lo else new
        below = rows > j + 1
        ba = b * (1.0 / a)
        um = jnp.where(below, u, jnp.where(rows == j + 1, ba, 0.0))
        vm = jnp.where(below, v, 0.0)
        strips = [s - (um * s[j:j + 1] + vm * s[j + 1:j + 2]) for s in strips]
        ra = lax.rsqrt(a)
        rd = lax.rsqrt(d - ba * b)
        scale = jnp.where(rows == j, ra, jnp.where(rows == j + 1, rd, scale))
    return [s * scale for s in strips]


def cholesky_inverse(work, size):
    n = work.shape[0]
    for k in range(n // size):
        r0 = k * size
        use = [0, 1, 2] if r0 < 128 else [1, 2, 3]
        strips = {i: work[r0:r0 + size, 128 * i:128 * (i + 1)] for i in use}
        off = r0 % 128
        base = strips[r0 // 128]
        cols = [jnp.broadcast_to(base[:, off + j:off + j + 1], (size, 128)) for j in range(size)]
        done = dict(zip(use, factor_block(cols, [strips[i] for i in use], size)))
        for i in use:
            if i >= 2:
                work[r0:r0 + size, 128 * i:128 * (i + 1)] = done[i]
        rest = r0 + size
        if rest == n:
            break
        low = (rest // 128) * 128
        pieces = {i: split3(done[i]) for i in use}
        ahead = [i for i in use if i < 2 and i * 128 >= low]
        h, m, l = [jnp.concatenate([pieces[i][t] for i in ahead], 1) for t in range(3)]
        left = jnp.concatenate([h, h, m, h, l, m], 0)
        for i in use:
            if i < 2 and (i + 1) * 128 <= rest:
                continue
            h, m, l = pieces[i]
            change = mm(left, jnp.concatenate([h, m, h, l, h, m], 0), TN)
            cols_i = slice(128 * i, 128 * (i + 1))
            work[rest:n, cols_i] = work[rest:n, cols_i] - change[rest - low:]


def basis_kernel(scale, gram_ref, image_hbm, out_ref, image, work, sem):
    copy = pltpu.make_async_copy(image_hbm, image, sem)
    copy.start()
    row = lax.broadcasted_iota(jnp.int32, (128, 128), 0)
    col = lax.broadcasted_iota(jnp.int32, (128, 128), 1)
    both = gram_ref[0:16, 0:8].reshape(128, 128)
    cross = gram_ref[16:32, 0:8].reshape(128, 128)
    last = gram_ref[0, 8:9]
    turned = both.T
    diag = row == col
    first = jnp.where(row >= col, both, turned)
    corner = jnp.where(diag, last, jnp.where(row < col, both, turned))
    row1 = lax.rsqrt(jnp.sum(jnp.where(diag, first, 0.0), axis=0, keepdims=True))
    row2 = lax.rsqrt(last)
    col1 = lax.rsqrt(jnp.sum(jnp.where(diag, first, 0.0), axis=1, keepdims=True))
    col2 = lax.rsqrt(jnp.sum(jnp.where(diag, corner, 0.0), axis=1, keepdims=True))
    eye = jnp.where(diag, 1.0, 0.0)
    zero = jnp.zeros((128, 128), F32)
    work[:128, 0:128] = first * col1 * row1
    work[:128, 128:256] = cross * col1 * row2
    work[128:, 128:256] = corner * col2 * row2
    work[:128, 256:384] = eye
    work[:128, 384:512] = zero
    work[128:, 256:384] = zero
    work[128:, 384:512] = eye
    cholesky_inverse(work, 16)
    factor = jnp.concatenate([work[:, 256:384] * (row1 * scale), work[:, 384:512] * (row2 * scale)], 1)
    fh, fl = split2(factor)
    copy.wait()
    hi, lo = split2(image[...])
    out_ref[...] = mm(hi, fh, NT) + (mm(hi, fl, NT) + mm(lo, fh, NT))


def basis_of(gram, image, scale):
    rows = image.shape[0]
    return pl.pallas_call(
        functools.partial(basis_kernel, scale),
        out_shape=jax.ShapeDtypeStruct((rows, K), F32),
        in_specs=[pl.BlockSpec(memory_space=pltpu.VMEM), pl.BlockSpec(memory_space=pl.ANY)],
        out_specs=pl.BlockSpec(memory_space=pltpu.VMEM),
        scratch_shapes=[
            pltpu.VMEM((rows, K), F32),
            pltpu.VMEM((K, 2 * K), F32),
            pltpu.SemaphoreType.DMA,
        ],
        compiler_params=pltpu.CompilerParams(vmem_limit_bytes=48 << 20),
        name="basis",
    )(gram, image)


def local(embeddings, start_basis):
    total_rows = embeddings.shape[0] * lax.axis_size("dp")
    image, gram = sums(embeddings, start_basis)
    return basis_of(gram, image, float(total_rows) ** 0.5)


def solution(mesh):
    in_specs = (P("dp", None), P("dp", None))
    out_specs = P("dp", None)
    return jax.shard_map(local, mesh=mesh, in_specs=in_specs, out_specs=out_specs, check_vma=False)
```

```python
import functools

import jax
import jax.numpy as jnp
from jax import lax
from jax.experimental import pallas as pl
from jax.experimental.pallas import tpu as pltpu
from jax.sharding import PartitionSpec as P

F32, BF16 = jnp.float32, jnp.bfloat16
NX, NZ, NY, NC = 4, 16, 4, 2
PLANE = NX * NY
D, K = 1024, 256
PARTS = 4
WIDE = D // PARTS
HALVES = 2
HALF = K // HALVES
OWN = D // NC
OWN_TILES = OWN // 128
BLOCK = 16
VMEM_BYTES = 60 << 20

PLANE_STEPS = sorted(
    [(dx, dy) for dx in range(NX) for dy in range(NY) if (dx, dy) != (0, 0)],
    key=lambda s: -(min(s[0], NX - s[0]) + min(s[1], NY - s[1])),
)
PLANE_CORE_STEPS = [(dx, dy, dc) for dx, dy in PLANE_STEPS for dc in range(NC)] + [(0, 0, 1)]
Z_STEPS = sorted(range(1, NZ), key=lambda d: -min(d, NZ - d))

NT = (((1,), (1,)), ((), ()))
NN = (((1,), (0,)), ((), ()))
TN = (((0,), (0,)), ((), ()))


def mm(a, b, dims):
    return lax.dot_general(a, b, dims, preferred_element_type=F32)


def split2(value):
    high = value.astype(BF16)
    return high, (value - high.astype(F32)).astype(BF16)


def split3(value):
    high = value.astype(BF16)
    rest = value - high.astype(F32)
    middle = rest.astype(BF16)
    return high, middle, (rest - middle.astype(F32)).astype(BF16)


def device(x, z, y, c):
    return ((x * NZ + z) * NY + y) * NC + c


def remote(src, dst, send, recv, target):
    return pltpu.make_async_remote_copy(
        src_ref=src,
        dst_ref=dst,
        send_sem=send,
        recv_sem=recv,
        device_id={"dp": target},
        device_id_type=pl.DeviceIdType.MESH,
    )


def offset(x, y, dx, dy):
    return ((x + dx) % NX) * NY + (y + dy) % NY


def gather_kernel(
    emb_hbm, start_hbm, image_hbm, gram_ref, first_ref,
    emb, emb_hi, emb_lo, start, give, core_in, part, plane_in, tiles, z_in, sketch,
    image, gram_part, gram_in_a, gram_in_b, gram_z_a, gram_z_b, gram_all,
    load_sem, core_s, core_r, xs, xr, zs, zr, ags, agr, bs, br, fs, fr,
    gas, gar, gbs, gbr, has, har, hbs, hbr, kas, kar, kbs, kbr, out_sem,
):
    me = lax.axis_index("dp")
    x, z, y, c = me // (NZ * NY * NC), (me // (NY * NC)) % NZ, (me // NC) % NY, me % NC
    p = x * NY + y
    sibling = device(x, z, y, 1 - c)
    around = [(0, 0)] + PLANE_STEPS

    def at(q, core):
        return device(q // NY, z, q % NY, core)

    places = [NC * (1 - c), NC * (1 - c) + 1, NC * c, NC * c + 1]

    def wide(i):
        return pl.ds(pl.multiple_of(places[i] * WIDE, WIDE), WIDE)

    loads = [pltpu.make_async_copy(start_hbm, start, load_sem.at[PARTS])]
    loads += [pltpu.make_async_copy(emb_hbm.at[:, wide(i)], emb.at[i], load_sem.at[i]) for i in range(PARTS)]
    for copy in loads:
        copy.start()

    barrier = pltpu.get_barrier_semaphore()
    greeted = [device(x, (z + step) % NZ, y, c) for step in Z_STEPS]
    greeted += [at(offset(x, y, dx, dy), (c + dc) % NC) for dx, dy, dc in PLANE_CORE_STEPS]
    for other in greeted:
        pl.semaphore_signal(barrier, inc=1, device_id={"dp": other}, device_id_type=pl.DeviceIdType.MESH)

    loads[0].wait()
    start_hi, start_lo = split2(start[...].T)

    def core_copy(i):
        return remote(give.at[i], core_in.at[i], core_s.at[i], core_r.at[i], sibling)

    for i in range(PARTS):
        loads[1 + i].wait()
        hi, lo = split2(emb[i])
        emb_hi[i] = hi
        emb_lo[i] = lo
        total = mm(start_hi, hi, NN) + (mm(start_hi, lo, NN) + mm(start_lo, hi, NN))
        total = total.reshape(HALVES, PLANE, 8, WIDE)
        if i < NC:
            give[i] = total
            if i == 0:
                pl.semaphore_wait(barrier, len(greeted))
            core_copy(i).start()
        else:
            j = i - NC
            core_copy(j).wait_recv()
            part[:, :, :, j * WIDE:(j + 1) * WIDE] = total + core_in[j]

    def plane_copy(h, o):
        q = offset(x, y, *PLANE_STEPS[o])
        return remote(part.at[h, q], plane_in.at[h, o], xs.at[h, o], xr.at[h, o], at(q, c))

    for h in range(HALVES):
        for o in range(PLANE - 1):
            plane_copy(h, o).start()

    def keeper(h, t):
        return 4 * t + NC * h + c

    def z_copy(h, t):
        step = (keeper(h, t) - z + NZ) % NZ
        return remote(tiles.at[h, t], z_in.at[step], zs.at[h, t], zr.at[step], device(x, keeper(h, t), y, c))

    for h in range(HALVES):
        for o in range(PLANE - 1):
            plane_copy(h, o).wait_recv()
        total = part[h, p]
        for o in range(PLANE - 1):
            total = total + plane_in[h, o]
        for t in range(OWN_TILES):
            tiles[h, t] = total[:, t * 128:(t + 1) * 128]
        for t in range(OWN_TILES):
            @pl.when(keeper(h, t) != z)
            def _(h=h, t=t):
                z_copy(h, t).start()

    def lanes(start, size):
        return pl.ds(pl.multiple_of(start, 128), size)

    def tile_of(h, t):
        return sketch.at[h, p, :, lanes(c * OWN + t * 128, 128)]

    mine = z // 4

    def z_out(h, step):
        return remote(tile_of(h, mine), tile_of(h, mine), ags.at[step], agr.at[h, mine], device(x, (z + step) % NZ, y, c))

    def keeps(h):
        return z % 4 == NC * h + c

    for h in range(HALVES):
        @pl.when(keeps(h))
        def _(h=h):
            for step in reversed(Z_STEPS):
                remote(tiles.at[0, 0], z_in.at[step], zs.at[0, 0], zr.at[step], me).wait_recv()
            total = tiles[h, mine]
            for step in range(1, NZ):
                total = total + z_in[step]
            sketch[h, p, :, lanes(c * OWN + mine * 128, 128)] = total
            for step in Z_STEPS:
                z_out(h, step).start()

    def block_of(h, q, core):
        return sketch.at[h, q, :, lanes(core * OWN, OWN)]

    def plane_out(h, o):
        q = offset(x, y, *PLANE_STEPS[o])
        return remote(block_of(h, p, c), block_of(h, p, c), bs.at[h, o], br.at[h, o], at(q, c))

    def source(o):
        if o == PLANE - 1:
            return p
        dx, dy = PLANE_STEPS[o]
        return offset(x, y, -dx, -dy)

    def forward(h, o):
        return remote(block_of(h, source(o), c), block_of(h, source(o), c), fs.at[h, o], fr.at[h, o], sibling)

    for h in range(HALVES):
        for t in range(OWN_TILES):
            @pl.when(keeper(h, t) != z)
            def _(h=h, t=t):
                remote(tile_of(h, t), tile_of(h, t), ags.at[0], agr.at[h, t], me).wait_recv()
        for o in range(PLANE - 1):
            plane_out(h, o).start()
        forward(h, PLANE - 1).start()

    def image_part(h, core):
        total = None
        for j in range(NC):
            i = (NC if core is c else 0) + j
            block = sketch[h, :, :, lanes(core * OWN + j * WIDE, WIDE)]
            hi, lo = split2(block.reshape(PLANE * 8, WIDE))
            term = mm(emb_hi[i], hi, NT) + (mm(emb_hi[i], lo, NT) + mm(emb_lo[i], hi, NT))
            total = term if total is None else total + term
        return total

    halves = []
    for h in range(HALVES):
        for o in reversed(range(PLANE - 1)):
            block = block_of(h, source(o), c)
            remote(block, block, bs.at[h, o], br.at[h, o], me).wait_recv()
            forward(h, o).start()
        halves.append(image_part(h, c))

    keeps_a = y % NC == c

    def gram_a(s):
        q = offset(x, y, *around[s])
        return remote(gram_part.at[0, q], gram_in_a.at[NC * s + c], gas.at[s], gar.at[NC * s + c], at(q, (q % NY) % NC))

    def gram_b(s, dc):
        q, core = offset(x, y, *around[s]), (c + dc) % NC
        return remote(gram_part.at[1 + core, q], gram_in_b.at[NC * s + c], gbs.at[NC * s + dc], gbr.at[NC * s + c], at(q, core))

    pairs = [(s, dc) for s in range(PLANE) for dc in range(NC) if (s, dc) != (0, 0)]

    turned = []
    for h in range(HALVES):
        for o in range(PLANE):
            block = block_of(h, source(o), 1 - c)
            remote(block, block, fs.at[h, o], fr.at[h, o], me).wait_recv()
        value = halves[h] + image_part(h, 1 - c)
        image[:, h * HALF:(h + 1) * HALF] = value
        turned.append(split2(value.T))
        bh, bl = split2(value)
        for g in range(h + 1):
            ah, al = turned[g]
            gram = mm(ah, bh, NN) + (mm(ah, bl, NN) + mm(al, bh, NN)) + mm(al, bl, NN)
            gram_part[h + g] = gram.reshape(PLANE, 8, 128)
        if h == 0:
            for s in range(1, PLANE):
                gram_a(s).start()

            @pl.when(jnp.logical_not(keeps_a))
            def _():
                gram_a(0).start()
        else:
            for s, dc in pairs:
                gram_b(s, dc).start()
    image_copy = pltpu.make_async_copy(image, image_hbm, out_sem)
    image_copy.start()

    def gram_z_copy(store, send, recv, step):
        return remote(store.at[z], store.at[z], send.at[step], recv.at[step], device(x, (z + step) % NZ, y, c))

    @pl.when(keeps_a)
    def _():
        total = gram_part[0, p]
        for s, dc in pairs:
            slot = NC * s + (c + dc) % NC
            remote(gram_part.at[0, 0], gram_in_a.at[slot], gas.at[0], gar.at[slot], me).wait_recv()
            total = total + gram_in_a[slot]
        gram_z_a[z] = total
        for step in Z_STEPS:
            gram_z_copy(gram_z_a, has, har, step).start()

    total = gram_part[1 + c, p]
    for s, dc in pairs:
        slot = NC * s + (c + dc) % NC
        remote(gram_part.at[0, 0], gram_in_b.at[slot], gbs.at[0], gbr.at[slot], me).wait_recv()
        total = total + gram_in_b[slot]
    gram_z_b[z] = total
    for step in Z_STEPS:
        gram_z_copy(gram_z_b, hbs, hbr, step).start()

    def z_sum(store, send, recv):
        for step in reversed(Z_STEPS):
            src = (z - step + NZ) % NZ
            remote(store.at[src], store.at[src], send.at[step], recv.at[step], me).wait_recv()
        total = store[0]
        for i in range(1, NZ):
            total = total + store[i]
        return total

    def gram_out_a(s, dc):
        block = gram_all.at[0, p]
        return remote(block, block, kas.at[NC * s + dc], kar.at[p], at(offset(x, y, *around[s]), (c + dc) % NC))

    def gram_out_b(s, dc):
        block = gram_all.at[1 + c, p]
        return remote(block, block, kbs.at[NC * s + dc], kbr.at[c, p], at(offset(x, y, *around[s]), (c + dc) % NC))

    @pl.when(keeps_a)
    def _():
        gram_all[0, p] = z_sum(gram_z_a, has, har)
        for s, dc in pairs:
            gram_out_a(s, dc).start()

    gram_all[1 + c, p] = z_sum(gram_z_b, hbs, hbr)
    for s, dc in pairs:
        gram_out_b(s, dc).start()

    for s in range(1, PLANE):
        q = offset(x, y, *around[s])
        remote(gram_all.at[0, q], gram_all.at[0, q], kas.at[0], kar.at[q], me).wait_recv()

    @pl.when(jnp.logical_not(keeps_a))
    def _():
        remote(gram_all.at[0, p], gram_all.at[0, p], kas.at[0], kar.at[p], me).wait_recv()

    first_ref[...] = first_inverse(gram_all[0].reshape(HALF, HALF))

    for s, dc in pairs:
        q, core = offset(x, y, *around[s]), (c + dc) % NC
        remote(gram_all.at[1 + core, q], gram_all.at[1 + core, q], kbs.at[0], kbr.at[core, q], me).wait_recv()
    gram_ref[...] = gram_all[1:3].reshape(NC, HALF, HALF)

    image_copy.wait()
    for i in range(NC):
        core_copy(i).wait_send()
    for h in range(HALVES):
        for o in range(PLANE - 1):
            plane_copy(h, o).wait_send()
            plane_out(h, o).wait_send()
        for o in range(PLANE):
            forward(h, o).wait_send()
        for t in range(OWN_TILES):
            @pl.when(keeper(h, t) != z)
            def _(h=h, t=t):
                z_copy(h, t).wait_send()

        @pl.when(keeps(h))
        def _(h=h):
            for step in Z_STEPS:
                z_out(h, step).wait_send()
    for s in range(1, PLANE):
        gram_a(s).wait_send()

    @pl.when(jnp.logical_not(keeps_a))
    def _():
        gram_a(0).wait_send()

    @pl.when(keeps_a)
    def _():
        for step in Z_STEPS:
            gram_z_copy(gram_z_a, has, har, step).wait_send()
        for s, dc in pairs:
            gram_out_a(s, dc).wait_send()
    for s, dc in pairs:
        gram_b(s, dc).wait_send()
        gram_out_b(s, dc).wait_send()
    for step in Z_STEPS:
        gram_z_copy(gram_z_b, hbs, hbr, step).wait_send()


def sums(embeddings, start_basis):
    rows = embeddings.shape[0]
    dma = lambda *n: pltpu.SemaphoreType.DMA(n)
    vmem = pltpu.VMEM
    return pl.pallas_call(
        gather_kernel,
        out_shape=(
            jax.ShapeDtypeStruct((rows, K), F32),
            jax.ShapeDtypeStruct((NC, HALF, HALF), F32),
            jax.ShapeDtypeStruct((HALF, HALF), F32),
        ),
        in_specs=[pl.BlockSpec(memory_space=pl.ANY)] * 2,
        out_specs=(pl.BlockSpec(memory_space=pl.ANY),) + (pl.BlockSpec(memory_space=pltpu.VMEM),) * 2,
        scratch_shapes=[
            vmem((PARTS, rows, WIDE), F32),
            vmem((PARTS, rows, WIDE), BF16),
            vmem((PARTS, rows, WIDE), BF16),
            vmem((rows, K), F32),
            vmem((NC, HALVES, PLANE, 8, WIDE), F32),
            vmem((NC, HALVES, PLANE, 8, WIDE), F32),
            vmem((HALVES, PLANE, 8, OWN), F32),
            vmem((HALVES, PLANE - 1, 8, OWN), F32),
            vmem((HALVES, OWN_TILES, 8, 128), F32),
            vmem((NZ, 8, 128), F32),
            vmem((HALVES, PLANE, 8, D), F32),
            vmem((rows, K), F32),
            vmem((3, PLANE, 8, 128), F32),
            vmem((32, 8, 128), F32),
            vmem((32, 8, 128), F32),
            vmem((NZ, 8, 128), F32),
            vmem((NZ, 8, 128), F32),
            vmem((3, PLANE, 8, 128), F32),
            dma(PARTS + 1),
            dma(NC), dma(NC),
            dma(HALVES, PLANE), dma(HALVES, PLANE),
            dma(HALVES, OWN_TILES), dma(NZ),
            dma(NZ), dma(HALVES, OWN_TILES),
            dma(HALVES, PLANE), dma(HALVES, PLANE),
            dma(HALVES, PLANE), dma(HALVES, PLANE),
            dma(PLANE), dma(32),
            dma(32), dma(32),
            dma(NZ), dma(NZ),
            dma(NZ), dma(NZ),
            dma(32), dma(PLANE),
            dma(32), dma(NC, PLANE),
            pltpu.SemaphoreType.DMA,
        ],
        compiler_params=pltpu.CompilerParams(
            collective_id=0, has_side_effects=True, vmem_limit_bytes=VMEM_BYTES
        ),
        name="sums",
    )(embeddings, start_basis)


def factor_block(cols, strips, size):
    rows = lax.broadcasted_iota(jnp.int32, (size, 128), 0)
    scale = jnp.zeros((size, 128), F32)
    for j in range(0, size, 2):
        cj, cn = cols[j], cols[j + 1]
        a, b, d = cj[j:j + 1], cj[j + 1:j + 2], cn[j + 1:j + 2]
        q = 1.0 / (a * d - b * b)
        aq, bq, dq = a * q, b * q, d * q
        u = cj * dq - cn * bq
        v = cn * aq - cj * bq
        for k in range(j + 2, size):
            lo = (k // 8) * 8
            new = cols[k][lo:] - (u[lo:] * cj[k:k + 1] + v[lo:] * cn[k:k + 1])
            cols[k] = jnp.concatenate([cols[k][:lo], new], 0) if lo else new
        below = rows > j + 1
        ba = b * (1.0 / a)
        um = jnp.where(below, u, jnp.where(rows == j + 1, ba, 0.0))
        vm = jnp.where(below, v, 0.0)
        strips = [s - (um * s[j:j + 1] + vm * s[j + 1:j + 2]) for s in strips]
        ra = lax.rsqrt(a)
        rd = lax.rsqrt(d - ba * b)
        scale = jnp.where(rows == j, ra, jnp.where(rows == j + 1, rd, scale))
    return [s * scale for s in strips]


LEFT = (0, 0, 1, 0, 2, 1)
RIGHT = (0, 1, 0, 2, 0, 1)


def stacked(pieces, order):
    return jnp.concatenate([pieces[i] for i in order], 0)


def eliminate(panels):
    size = BLOCK
    done = []
    for k in range(HALF // size):
        off = k * size
        strips = [panel[:size] for panel in panels]
        cols = [jnp.broadcast_to(strips[0][:, off + j:off + j + 1], (size, 128)) for j in range(size)]
        strips = factor_block(cols, strips, size)
        done.append(strips[1:])
        if off + size == HALF:
            break
        pieces = [split3(s) for s in strips]
        left = stacked(pieces[0], LEFT)
        right = jnp.concatenate([stacked(piece, RIGHT) for piece in pieces], 1)
        change = mm(left, right, TN)
        panels = [
            panel[size:] - change[off + size:, 128 * i:128 * (i + 1)] for i, panel in enumerate(panels)
        ]
    return [jnp.concatenate([strips[i] for strips in done], 0) for i in range(len(panels) - 1)]


def mm6(a, b, dims):
    ah, am, al = split3(a)
    bh, bm, bl = split3(b)
    return mm(ah, bh, dims) + (mm(ah, bm, dims) + mm(am, bh, dims)) + (mm(am, bm, dims) + (mm(ah, bl, dims) + mm(al, bh, dims)))


def diagonal():
    return lax.broadcasted_iota(jnp.int32, (HALF, HALF), 0) == lax.broadcasted_iota(jnp.int32, (HALF, HALF), 1)


def diagonal_scales(value):
    entries = jnp.where(diagonal(), value, 0.0)
    return (
        lax.rsqrt(jnp.sum(entries, axis=1, keepdims=True)),
        lax.rsqrt(jnp.sum(entries, axis=0, keepdims=True)),
    )


def first_inverse(aa):
    col, row = diagonal_scales(aa)
    (inverse,) = eliminate([aa * col * row, jnp.where(diagonal(), 1.0, 0.0)])
    return inverse * row


def basis_kernel(scale, gram_ref, first_ref, image_hbm, out_ref, image, sem):
    copy = pltpu.make_async_copy(image_hbm, image, sem)
    copy.start()
    first = first_ref[...]
    ab, bb = gram_ref[0], gram_ref[1]
    col, row = diagonal_scales(bb)
    cross = mm6(first, ab * row, NN)
    turned = cross.T
    rest = bb * col * row - mm6(turned, cross, NN)
    lower = mm6(turned, first, NN)
    copy.wait()
    fh, fl = split2(first * scale)
    ih, il = split2(image[:, :HALF])
    out_ref[:, :HALF] = mm(ih, fh, NT) + (mm(ih, fl, NT) + mm(il, fh, NT))
    below, second = eliminate([rest, -lower, jnp.where(diagonal(), 1.0, 0.0)])
    gh, gl = split2(jnp.concatenate([below, second * row], 1) * scale)
    hi, lo = split2(image[...])
    out_ref[:, HALF:] = mm(hi, gh, NT) + (mm(hi, gl, NT) + mm(lo, gh, NT))


def basis_of(gram, first, image, scale):
    rows = image.shape[0]
    in_vmem = pl.BlockSpec(memory_space=pltpu.VMEM)
    return pl.pallas_call(
        functools.partial(basis_kernel, scale),
        out_shape=jax.ShapeDtypeStruct((rows, K), F32),
        in_specs=[in_vmem, in_vmem, pl.BlockSpec(memory_space=pl.ANY)],
        out_specs=in_vmem,
        scratch_shapes=[pltpu.VMEM((rows, K), F32), pltpu.SemaphoreType.DMA],
        compiler_params=pltpu.CompilerParams(vmem_limit_bytes=VMEM_BYTES),
        name="basis",
    )(gram, first, image)


def local(embeddings, start_basis):
    total_rows = embeddings.shape[0] * lax.axis_size("dp")
    image, gram, first = sums(embeddings, start_basis)
    return basis_of(gram, first, image, float(total_rows) ** 0.5)


def solution(mesh):
    in_specs = (P("dp", None), P("dp", None))
    out_specs = P("dp", None)
    return jax.shard_map(local, mesh=mesh, in_specs=in_specs, out_specs=out_specs, check_vma=False)
```

```python
import functools

import jax
import jax.numpy as jnp
from jax import lax
from jax.experimental import pallas as pl
from jax.experimental.pallas import tpu as pltpu
from jax.sharding import PartitionSpec as P

F32, BF16 = jnp.float32, jnp.bfloat16
NX, NZ, NY, NC = 4, 16, 4, 2
PLANE = NX * NY
D, K = 1024, 256
PARTS = 4
WIDE = D // PARTS
HALVES = 2
HALF = K // HALVES
OWN = D // NC
OWN_TILES = OWN // 128
BLOCK = 16
VMEM_BYTES = 60 << 20

PLANE_STEPS = sorted(
    [(dx, dy) for dx in range(NX) for dy in range(NY) if (dx, dy) != (0, 0)],
    key=lambda s: -(min(s[0], NX - s[0]) + min(s[1], NY - s[1])),
)
PLANE_CORE_STEPS = [(dx, dy, dc) for dx, dy in PLANE_STEPS for dc in range(NC)] + [(0, 0, 1)]
Z_STEPS = sorted(range(1, NZ), key=lambda d: -min(d, NZ - d))

NT = (((1,), (1,)), ((), ()))
NN = (((1,), (0,)), ((), ()))
TN = (((0,), (0,)), ((), ()))


def mm(a, b, dims):
    return lax.dot_general(a, b, dims, preferred_element_type=F32)


def split2(value):
    high = value.astype(BF16)
    return high, (value - high.astype(F32)).astype(BF16)


def split3(value):
    high = value.astype(BF16)
    rest = value - high.astype(F32)
    middle = rest.astype(BF16)
    return high, middle, (rest - middle.astype(F32)).astype(BF16)


def device(x, z, y, c):
    return ((x * NZ + z) * NY + y) * NC + c


def remote(src, dst, send, recv, target):
    return pltpu.make_async_remote_copy(
        src_ref=src,
        dst_ref=dst,
        send_sem=send,
        recv_sem=recv,
        device_id={"dp": target},
        device_id_type=pl.DeviceIdType.MESH,
    )


def offset(x, y, dx, dy):
    return ((x + dx) % NX) * NY + (y + dy) % NY


def gather_kernel(
    emb_hbm, start_hbm, image_hbm, gram_ref, first_ref,
    emb, emb_hi, emb_lo, start, give, core_in, part, plane_in, tiles, z_in, sketch,
    image, gram_part, gram_in_a, gram_in_b, gram_z_a, gram_z_b, gram_all,
    load_sem, core_s, core_r, xs, xr, zs, zr, ags, agr, bs, br, fs, fr,
    gas, gar, gbs, gbr, has, har, hbs, hbr, kas, kar, kbs, kbr, out_sem, relay,
):
    me = lax.axis_index("dp")
    x, z, y, c = me // (NZ * NY * NC), (me // (NY * NC)) % NZ, (me // NC) % NY, me % NC
    p = x * NY + y
    sibling = device(x, z, y, 1 - c)
    around = [(0, 0)] + PLANE_STEPS

    def at(q, core):
        return device(q // NY, z, q % NY, core)

    places = [NC * (1 - c), NC * (1 - c) + 1, NC * c, NC * c + 1]

    def wide(i):
        return pl.ds(pl.multiple_of(places[i] * WIDE, WIDE), WIDE)

    loads = [pltpu.make_async_copy(start_hbm, start, load_sem.at[PARTS])]
    loads += [pltpu.make_async_copy(emb_hbm.at[:, wide(i)], emb.at[i], load_sem.at[i]) for i in range(PARTS)]
    for copy in loads:
        copy.start()

    barrier = pltpu.get_barrier_semaphore()
    greeted = [device(x, (z + step) % NZ, y, c) for step in Z_STEPS if min(step, NZ - step) <= NZ // 4]
    greeted += [at(offset(x, y, dx, dy), (c + dc) % NC) for dx, dy, dc in PLANE_CORE_STEPS]
    for other in greeted:
        pl.semaphore_signal(barrier, inc=1, device_id={"dp": other}, device_id_type=pl.DeviceIdType.MESH)

    loads[0].wait()
    start_hi, start_lo = split2(start[...].T)

    def core_copy(i):
        return remote(give.at[i], core_in.at[i], core_s.at[i], core_r.at[i], sibling)

    for i in range(PARTS):
        loads[1 + i].wait()
        hi, lo = split2(emb[i])
        emb_hi[i] = hi
        emb_lo[i] = lo
        total = mm(start_hi, hi, NN) + (mm(start_hi, lo, NN) + mm(start_lo, hi, NN))
        total = total.reshape(HALVES, PLANE, 8, WIDE)
        if i < NC:
            give[i] = total
            if i == 0:
                pl.semaphore_wait(barrier, len(greeted))
                for step in (NZ // 4, NZ - NZ // 4):
                    pl.semaphore_signal(relay, inc=1, device_id={"dp": device(x, (z + step) % NZ, y, c)}, device_id_type=pl.DeviceIdType.MESH)
            core_copy(i).start()
        else:
            j = i - NC
            core_copy(j).wait_recv()
            part[:, :, :, j * WIDE:(j + 1) * WIDE] = total + core_in[j]

    def plane_copy(h, o):
        q = offset(x, y, *PLANE_STEPS[o])
        return remote(part.at[h, q], plane_in.at[h, o], xs.at[h, o], xr.at[h, o], at(q, c))

    for h in range(HALVES):
        for o in range(PLANE - 1):
            plane_copy(h, o).start()

    pl.semaphore_wait(relay, 2)

    def keeper(h, t):
        return 4 * t + NC * h + c

    def z_copy(h, t):
        step = (keeper(h, t) - z + NZ) % NZ
        return remote(tiles.at[h, t], z_in.at[step], zs.at[h, t], zr.at[step], device(x, keeper(h, t), y, c))

    for h in range(HALVES):
        for o in range(PLANE - 1):
            plane_copy(h, o).wait_recv()
        total = part[h, p]
        for o in range(PLANE - 1):
            total = total + plane_in[h, o]
        for t in range(OWN_TILES):
            tiles[h, t] = total[:, t * 128:(t + 1) * 128]
        for t in range(OWN_TILES):
            @pl.when(keeper(h, t) != z)
            def _(h=h, t=t):
                z_copy(h, t).start()

    def lanes(start, size):
        return pl.ds(pl.multiple_of(start, 128), size)

    def tile_of(h, t):
        return sketch.at[h, p, :, lanes(c * OWN + t * 128, 128)]

    mine = z // 4

    def z_out(h, step):
        return remote(tile_of(h, mine), tile_of(h, mine), ags.at[step], agr.at[h, mine], device(x, (z + step) % NZ, y, c))

    def keeps(h):
        return z % 4 == NC * h + c

    for h in range(HALVES):
        @pl.when(keeps(h))
        def _(h=h):
            for step in reversed(Z_STEPS):
                remote(tiles.at[0, 0], z_in.at[step], zs.at[0, 0], zr.at[step], me).wait_recv()
            total = tiles[h, mine]
            for step in range(1, NZ):
                total = total + z_in[step]
            sketch[h, p, :, lanes(c * OWN + mine * 128, 128)] = total
            for step in Z_STEPS:
                z_out(h, step).start()

    def block_of(h, q, core):
        return sketch.at[h, q, :, lanes(core * OWN, OWN)]

    def plane_out(h, o):
        q = offset(x, y, *PLANE_STEPS[o])
        return remote(block_of(h, p, c), block_of(h, p, c), bs.at[h, o], br.at[h, o], at(q, c))

    def source(o):
        if o == PLANE - 1:
            return p
        dx, dy = PLANE_STEPS[o]
        return offset(x, y, -dx, -dy)

    def forward(h, o):
        return remote(block_of(h, source(o), c), block_of(h, source(o), c), fs.at[h, o], fr.at[h, o], sibling)

    for h in range(HALVES):
        for t in range(OWN_TILES):
            @pl.when(keeper(h, t) != z)
            def _(h=h, t=t):
                remote(tile_of(h, t), tile_of(h, t), ags.at[0], agr.at[h, t], me).wait_recv()
        for o in range(PLANE - 1):
            plane_out(h, o).start()
        forward(h, PLANE - 1).start()

    def image_part(h, core):
        total = None
        for j in range(NC):
            i = (NC if core is c else 0) + j
            block = sketch[h, :, :, lanes(core * OWN + j * WIDE, WIDE)]
            hi, lo = split2(block.reshape(HALF, WIDE))
            both = mm(jnp.concatenate([hi, lo], 0), emb_hi[i], NT)
            term = both[:HALF] + (both[HALF:] + mm(hi, emb_lo[i], NT))
            total = term if total is None else total + term
        return total

    halves = []
    for h in range(HALVES):
        for o in reversed(range(PLANE - 1)):
            block = block_of(h, source(o), c)
            remote(block, block, bs.at[h, o], br.at[h, o], me).wait_recv()
            forward(h, o).start()
        halves.append(image_part(h, c))

    keeps_a = y % NC == c

    def gram_a(s):
        q = offset(x, y, *around[s])
        return remote(gram_part.at[0, q], gram_in_a.at[NC * s + c], gas.at[s], gar.at[NC * s + c], at(q, (q % NY) % NC))

    def gram_b(s, dc):
        q, core = offset(x, y, *around[s]), (c + dc) % NC
        return remote(gram_part.at[1 + core, q], gram_in_b.at[NC * s + c], gbs.at[NC * s + dc], gbr.at[NC * s + c], at(q, core))

    pairs = [(s, dc) for s in range(PLANE) for dc in range(NC) if (s, dc) != (0, 0)]

    pieces = []
    for h in range(HALVES):
        for o in range(PLANE):
            block = block_of(h, source(o), 1 - c)
            remote(block, block, fs.at[h, o], fr.at[h, o], me).wait_recv()
        halves[h] = halves[h] + image_part(h, 1 - c)
        pieces += split2(halves[h])
        gram = mm(jnp.concatenate(pieces[-2:], 0), jnp.concatenate(pieces, 0), NT)
        gram = gram[:HALF] + gram[HALF:]
        for g in range(h + 1):
            block = gram[:, g * K:g * K + HALF] + gram[:, g * K + HALF:(g + 1) * K]
            gram_part[h + g] = block.reshape(PLANE, 8, 128)
        if h == 0:
            for s in range(1, PLANE):
                gram_a(s).start()

            @pl.when(jnp.logical_not(keeps_a))
            def _():
                gram_a(0).start()
        else:
            for s, dc in pairs:
                gram_b(s, dc).start()

    def gram_z_copy(store, send, recv, step):
        return remote(store.at[z], store.at[z], send.at[step], recv.at[step], device(x, (z + step) % NZ, y, c))

    @pl.when(keeps_a)
    def _():
        total = gram_part[0, p]
        for s, dc in pairs:
            slot = NC * s + (c + dc) % NC
            remote(gram_part.at[0, 0], gram_in_a.at[slot], gas.at[0], gar.at[slot], me).wait_recv()
            total = total + gram_in_a[slot]
        gram_z_a[z] = total
        for step in Z_STEPS:
            gram_z_copy(gram_z_a, has, har, step).start()

    total = gram_part[1 + c, p]
    for s, dc in pairs:
        slot = NC * s + (c + dc) % NC
        remote(gram_part.at[0, 0], gram_in_b.at[slot], gbs.at[0], gbr.at[slot], me).wait_recv()
        total = total + gram_in_b[slot]
    gram_z_b[z] = total
    for step in Z_STEPS:
        gram_z_copy(gram_z_b, hbs, hbr, step).start()

    image[...] = jnp.concatenate(halves, 0).T
    image_copy = pltpu.make_async_copy(image, image_hbm, out_sem)
    image_copy.start()
    for i in range(NC):
        core_copy(i).wait_send()
    for h in range(HALVES):
        for o in range(PLANE - 1):
            plane_copy(h, o).wait_send()
            plane_out(h, o).wait_send()
        for o in range(PLANE):
            forward(h, o).wait_send()
        for t in range(OWN_TILES):
            @pl.when(keeper(h, t) != z)
            def _(h=h, t=t):
                z_copy(h, t).wait_send()

        @pl.when(keeps(h))
        def _(h=h):
            for step in Z_STEPS:
                z_out(h, step).wait_send()
    for s in range(1, PLANE):
        gram_a(s).wait_send()

    @pl.when(jnp.logical_not(keeps_a))
    def _():
        gram_a(0).wait_send()

    for s, dc in pairs:
        gram_b(s, dc).wait_send()

    def z_sum(store, send, recv):
        for step in reversed(Z_STEPS):
            src = (z - step + NZ) % NZ
            remote(store.at[src], store.at[src], send.at[step], recv.at[step], me).wait_recv()
        total = store[0]
        for i in range(1, NZ):
            total = total + store[i]
        return total

    def gram_out_a(s, dc):
        block = gram_all.at[0, p]
        return remote(block, block, kas.at[NC * s + dc], kar.at[p], at(offset(x, y, *around[s]), (c + dc) % NC))

    def gram_out_b(s, dc):
        block = gram_all.at[1 + c, p]
        return remote(block, block, kbs.at[NC * s + dc], kbr.at[c, p], at(offset(x, y, *around[s]), (c + dc) % NC))

    @pl.when(keeps_a)
    def _():
        gram_all[0, p] = z_sum(gram_z_a, has, har)
        for s, dc in pairs:
            gram_out_a(s, dc).start()

    gram_all[1 + c, p] = z_sum(gram_z_b, hbs, hbr)
    for s, dc in pairs:
        gram_out_b(s, dc).start()

    for s in range(1, PLANE):
        q = offset(x, y, *around[s])
        remote(gram_all.at[0, q], gram_all.at[0, q], kas.at[0], kar.at[q], me).wait_recv()

    @pl.when(jnp.logical_not(keeps_a))
    def _():
        remote(gram_all.at[0, p], gram_all.at[0, p], kas.at[0], kar.at[p], me).wait_recv()

    first_ref[...] = first_inverse(gram_all[0].reshape(HALF, HALF))

    @pl.when(keeps_a)
    def _():
        for step in Z_STEPS:
            gram_z_copy(gram_z_a, has, har, step).wait_send()
        for s, dc in pairs:
            gram_out_a(s, dc).wait_send()

    for step in Z_STEPS:
        gram_z_copy(gram_z_b, hbs, hbr, step).wait_send()
    for s, dc in pairs:
        gram_out_b(s, dc).wait_send()
    image_copy.wait()

    for s, dc in pairs:
        q, core = offset(x, y, *around[s]), (c + dc) % NC
        remote(gram_all.at[1 + core, q], gram_all.at[1 + core, q], kbs.at[0], kbr.at[core, q], me).wait_recv()
    gram_ref[...] = gram_all[1:3].reshape(NC, HALF, HALF)


def sums(embeddings, start_basis):
    rows = embeddings.shape[0]
    dma = lambda *n: pltpu.SemaphoreType.DMA(n)
    vmem = pltpu.VMEM
    return pl.pallas_call(
        gather_kernel,
        out_shape=(
            jax.ShapeDtypeStruct((rows, K), F32),
            jax.ShapeDtypeStruct((NC, HALF, HALF), F32),
            jax.ShapeDtypeStruct((HALF, HALF), F32),
        ),
        in_specs=[pl.BlockSpec(memory_space=pl.ANY)] * 2,
        out_specs=(pl.BlockSpec(memory_space=pl.ANY),) + (pl.BlockSpec(memory_space=pltpu.VMEM),) * 2,
        scratch_shapes=[
            vmem((PARTS, rows, WIDE), F32),
            vmem((PARTS, rows, WIDE), BF16),
            vmem((PARTS, rows, WIDE), BF16),
            vmem((rows, K), F32),
            vmem((NC, HALVES, PLANE, 8, WIDE), F32),
            vmem((NC, HALVES, PLANE, 8, WIDE), F32),
            vmem((HALVES, PLANE, 8, OWN), F32),
            vmem((HALVES, PLANE - 1, 8, OWN), F32),
            vmem((HALVES, OWN_TILES, 8, 128), F32),
            vmem((NZ, 8, 128), F32),
            vmem((HALVES, PLANE, 8, D), F32),
            vmem((rows, K), F32),
            vmem((3, PLANE, 8, 128), F32),
            vmem((32, 8, 128), F32),
            vmem((32, 8, 128), F32),
            vmem((NZ, 8, 128), F32),
            vmem((NZ, 8, 128), F32),
            vmem((3, PLANE, 8, 128), F32),
            dma(PARTS + 1),
            dma(NC), dma(NC),
            dma(HALVES, PLANE), dma(HALVES, PLANE),
            dma(HALVES, OWN_TILES), dma(NZ),
            dma(NZ), dma(HALVES, OWN_TILES),
            dma(HALVES, PLANE), dma(HALVES, PLANE),
            dma(HALVES, PLANE), dma(HALVES, PLANE),
            dma(PLANE), dma(32),
            dma(32), dma(32),
            dma(NZ), dma(NZ),
            dma(NZ), dma(NZ),
            dma(32), dma(PLANE),
            dma(32), dma(NC, PLANE),
            pltpu.SemaphoreType.DMA,
            pltpu.SemaphoreType.REGULAR,
        ],
        compiler_params=pltpu.CompilerParams(
            collective_id=0, has_side_effects=True, vmem_limit_bytes=VMEM_BYTES
        ),
        name="sums",
    )(embeddings, start_basis)


def factor_block(cols, strips, size):
    rows = lax.broadcasted_iota(jnp.int32, (size, 128), 0)
    scale = jnp.zeros((size, 128), F32)
    for j in range(0, size, 2):
        cj, cn = cols[j], cols[j + 1]
        a, b, d = cj[j:j + 1], cj[j + 1:j + 2], cn[j + 1:j + 2]
        q = 1.0 / (a * d - b * b)
        aq, bq, dq = a * q, b * q, d * q
        u = cj * dq - cn * bq
        v = cn * aq - cj * bq
        for k in range(j + 2, size):
            lo = (k // 8) * 8
            new = cols[k][lo:] - (u[lo:] * cj[k:k + 1] + v[lo:] * cn[k:k + 1])
            cols[k] = jnp.concatenate([cols[k][:lo], new], 0) if lo else new
        below = rows > j + 1
        ba = b * (1.0 / a)
        um = jnp.where(below, u, jnp.where(rows == j + 1, ba, 0.0))
        vm = jnp.where(below, v, 0.0)
        strips = [s - (um * s[j:j + 1] + vm * s[j + 1:j + 2]) for s in strips]
        ra = lax.rsqrt(a)
        rd = lax.rsqrt(d - ba * b)
        scale = jnp.where(rows == j, ra, jnp.where(rows == j + 1, rd, scale))
    return [s * scale for s in strips]


LEFT = (0, 0, 1, 0, 2, 1)
RIGHT = (0, 1, 0, 2, 0, 1)


def stacked(pieces, order):
    return jnp.concatenate([pieces[i] for i in order], 0)


def eliminate(panels):
    size = BLOCK
    done = []
    for k in range(HALF // size):
        off = k * size
        strips = [panel[:size] for panel in panels]
        cols = [jnp.broadcast_to(strips[0][:, off + j:off + j + 1], (size, 128)) for j in range(size)]
        strips = factor_block(cols, strips, size)
        done.append(strips[1:])
        if off + size == HALF:
            break
        pieces = [split3(s) for s in strips]
        left = stacked(pieces[0], LEFT)
        right = jnp.concatenate([stacked(piece, RIGHT) for piece in pieces], 1)
        change = mm(left, right, TN)
        panels = [
            panel[size:] - change[off + size:, 128 * i:128 * (i + 1)] for i, panel in enumerate(panels)
        ]
    return [jnp.concatenate([strips[i] for strips in done], 0) for i in range(len(panels) - 1)]


def mm6(a, b, dims):
    ah, am, al = split3(a)
    bh, bm, bl = split3(b)
    return mm(ah, bh, dims) + (mm(ah, bm, dims) + mm(am, bh, dims)) + (mm(am, bm, dims) + (mm(ah, bl, dims) + mm(al, bh, dims)))


def diagonal():
    return lax.broadcasted_iota(jnp.int32, (HALF, HALF), 0) == lax.broadcasted_iota(jnp.int32, (HALF, HALF), 1)


def diagonal_scales(value):
    entries = jnp.where(diagonal(), value, 0.0)
    return (
        lax.rsqrt(jnp.sum(entries, axis=1, keepdims=True)),
        lax.rsqrt(jnp.sum(entries, axis=0, keepdims=True)),
    )


def first_inverse(aa):
    col, row = diagonal_scales(aa)
    (inverse,) = eliminate([aa * col * row, jnp.where(diagonal(), 1.0, 0.0)])
    return inverse * row


def basis_kernel(scale, gram_ref, first_ref, image_hbm, out_ref, image, sem):
    copy = pltpu.make_async_copy(image_hbm, image, sem)
    copy.start()
    first = first_ref[...]
    ba, bb = gram_ref[0], gram_ref[1]
    col, row = diagonal_scales(bb)
    cross = mm6(ba * col, first, NT)
    rest = bb * col * row - mm6(cross, cross, NT)
    lower = mm6(cross, first, NN)
    copy.wait()
    fh, fl = split2(first * scale)
    ih, il = split2(image[:, :HALF])
    out_ref[:, :HALF] = mm(ih, fh, NT) + (mm(ih, fl, NT) + mm(il, fh, NT))
    below, second = eliminate([rest, -lower, jnp.where(diagonal(), 1.0, 0.0)])
    gh, gl = split2(jnp.concatenate([below, second * row], 1) * scale)
    hi, lo = split2(image[...])
    out_ref[:, HALF:] = mm(hi, gh, NT) + (mm(hi, gl, NT) + mm(lo, gh, NT))


def basis_of(gram, first, image, scale):
    rows = image.shape[0]
    in_vmem = pl.BlockSpec(memory_space=pltpu.VMEM)
    return pl.pallas_call(
        functools.partial(basis_kernel, scale),
        out_shape=jax.ShapeDtypeStruct((rows, K), F32),
        in_specs=[in_vmem, in_vmem, pl.BlockSpec(memory_space=pl.ANY)],
        out_specs=in_vmem,
        scratch_shapes=[pltpu.VMEM((rows, K), F32), pltpu.SemaphoreType.DMA],
        compiler_params=pltpu.CompilerParams(vmem_limit_bytes=VMEM_BYTES),
        name="basis",
    )(gram, first, image)


def local(embeddings, start_basis):
    total_rows = embeddings.shape[0] * lax.axis_size("dp")
    image, gram, first = sums(embeddings, start_basis)
    return basis_of(gram, first, image, float(total_rows) ** 0.5)


def solution(mesh):
    in_specs = (P("dp", None), P("dp", None))
    out_specs = P("dp", None)
    return jax.shard_map(local, mesh=mesh, in_specs=in_specs, out_specs=out_specs, check_vma=False)
```

```python
import functools

import jax
import jax.numpy as jnp
from jax import lax
from jax.experimental import pallas as pl
from jax.experimental.pallas import tpu as pltpu
from jax.sharding import PartitionSpec as P

F32, BF16 = jnp.float32, jnp.bfloat16
NX, NZ, NY, NC = 4, 16, 4, 2
PLANE = NX * NY
D, K = 1024, 256
PARTS = 4
WIDE = D // PARTS
HALVES = 2
HALF = K // HALVES
OWN = D // NC
OWN_TILES = OWN // 128
BLOCK = 16
VMEM_BYTES = 60 << 20

PLANE_STEPS = sorted(
    [(dx, dy) for dx in range(NX) for dy in range(NY) if (dx, dy) != (0, 0)],
    key=lambda s: -(min(s[0], NX - s[0]) + min(s[1], NY - s[1])),
)
PLANE_CORE_STEPS = [(dx, dy, dc) for dx, dy in PLANE_STEPS for dc in range(NC)] + [(0, 0, 1)]
Z_STEPS = sorted(range(1, NZ), key=lambda d: -min(d, NZ - d))

NT = (((1,), (1,)), ((), ()))
NN = (((1,), (0,)), ((), ()))
TN = (((0,), (0,)), ((), ()))


def mm(a, b, dims):
    return lax.dot_general(a, b, dims, preferred_element_type=F32)


def split2(value):
    high = value.astype(BF16)
    return high, (value - high.astype(F32)).astype(BF16)


def split3(value):
    high = value.astype(BF16)
    rest = value - high.astype(F32)
    middle = rest.astype(BF16)
    return high, middle, (rest - middle.astype(F32)).astype(BF16)


def device(x, z, y, c):
    return ((x * NZ + z) * NY + y) * NC + c


def remote(src, dst, send, recv, target):
    return pltpu.make_async_remote_copy(
        src_ref=src,
        dst_ref=dst,
        send_sem=send,
        recv_sem=recv,
        device_id={"dp": target},
        device_id_type=pl.DeviceIdType.MESH,
    )


def offset(x, y, dx, dy):
    return ((x + dx) % NX) * NY + (y + dy) % NY


def landed(ref, sem):
    pltpu.make_async_copy(ref, ref, sem).wait()


def gather_kernel(
    emb_hbm, start_hbm, image_hbm, gram_ref, first_ref,
    emb, emb_hi, emb_lo, start, give, core_in, part, plane_in, tiles, z_in, sketch,
    image, gram_part, gram_in_a, gram_in_b, gram_z_a, gram_z_b, gram_all,
    load_sem, core_s, core_r, xs, xr, zs, zr, ags, agr, bs, br, fs, fr,
    gas, gar, gbs, gbr, has, har, hbs, hbr, kas, kar, kbs, kbr, out_sem, relay,
):
    me = lax.axis_index("dp")
    x, z, y, c = me // (NZ * NY * NC), (me // (NY * NC)) % NZ, (me // NC) % NY, me % NC
    p = x * NY + y
    sibling = device(x, z, y, 1 - c)
    around = [(0, 0)] + PLANE_STEPS

    def at(q, core):
        return device(q // NY, z, q % NY, core)

    places = [NC * (1 - c), NC * (1 - c) + 1, NC * c, NC * c + 1]

    def wide(i):
        return pl.ds(pl.multiple_of(places[i] * WIDE, WIDE), WIDE)

    loads = [pltpu.make_async_copy(start_hbm, start, load_sem.at[PARTS])]
    loads += [pltpu.make_async_copy(emb_hbm.at[:, wide(i)], emb.at[i], load_sem.at[i]) for i in range(PARTS)]
    for copy in loads:
        copy.start()

    barrier = pltpu.get_barrier_semaphore()
    greeted = [device(x, (z + step) % NZ, y, c) for step in Z_STEPS if min(step, NZ - step) <= NZ // 4]
    greeted += [at(offset(x, y, dx, dy), (c + dc) % NC) for dx, dy, dc in PLANE_CORE_STEPS]
    for other in greeted:
        pl.semaphore_signal(barrier, inc=1, device_id={"dp": other}, device_id_type=pl.DeviceIdType.MESH)

    loads[0].wait()
    start_hi, start_lo = split2(start[...].T)

    for i in range(PARTS):
        loads[1 + i].wait()
        hi, lo = split2(emb[i])
        emb_hi[i] = hi
        emb_lo[i] = lo
        total = mm(start_hi, hi, NN) + (mm(start_hi, lo, NN) + mm(start_lo, hi, NN))
        store, j = (give, i) if i < NC else (part, i - NC)
        store[:, :, :, j * WIDE:(j + 1) * WIDE] = total.reshape(HALVES, PLANE, 8, WIDE)

    pl.semaphore_wait(barrier, len(greeted))
    for step in (NZ // 4, NZ - NZ // 4):
        pl.semaphore_signal(relay, inc=1, device_id={"dp": device(x, (z + step) % NZ, y, c)}, device_id_type=pl.DeviceIdType.MESH)

    def core_copy(h):
        return remote(give.at[h], core_in.at[h], core_s.at[h], core_r.at[h], sibling)

    def plane_copy(h, o):
        q = offset(x, y, *PLANE_STEPS[o])
        return remote(part.at[h, q], plane_in.at[h, o], xs.at[h], xr.at[h], at(q, c))

    for h in range(HALVES):
        core_copy(h).start()
    for h in range(HALVES):
        core_copy(h).wait_recv()
        part[h] = part[h] + core_in[h]
        for o in range(PLANE - 1):
            plane_copy(h, o).start()

    pl.semaphore_wait(relay, 2)

    def keeper(h, t):
        return 4 * t + NC * h + c

    def z_copy(h, t):
        step = (keeper(h, t) - z + NZ) % NZ
        return remote(tiles.at[h, t], z_in.at[step], zs.at[h, t], zr.at[0], device(x, keeper(h, t), y, c))

    for h in range(HALVES):
        landed(plane_in.at[h], xr.at[h])
        total = part[h, p]
        for o in range(PLANE - 1):
            total = total + plane_in[h, o]
        for t in range(OWN_TILES):
            tiles[h, t] = total[:, t * 128:(t + 1) * 128]
        for t in range(OWN_TILES):
            @pl.when(keeper(h, t) != z)
            def _(h=h, t=t):
                z_copy(h, t).start()

    def lanes(start, size):
        return pl.ds(pl.multiple_of(start, 128), size)

    def tile_of(h, t):
        return sketch.at[h, p, :, lanes(c * OWN + t * 128, 128)]

    mine = z // 4

    def z_out(h, step):
        return remote(tile_of(h, mine), tile_of(h, mine), ags.at[0], agr.at[h, mine], device(x, (z + step) % NZ, y, c))

    def keeps(h):
        return z % 4 == NC * h + c

    for h in range(HALVES):
        @pl.when(keeps(h))
        def _(h=h):
            landed(z_in.at[pl.ds(1, NZ - 1)], zr.at[0])
            total = tiles[h, mine]
            for step in range(1, NZ):
                total = total + z_in[step]
            sketch[h, p, :, lanes(c * OWN + mine * 128, 128)] = total
            for step in Z_STEPS:
                z_out(h, step).start()

    def block_of(h, q, core):
        return sketch.at[h, q, :, lanes(core * OWN, OWN)]

    def plane_out(h, o):
        q = offset(x, y, *PLANE_STEPS[o])
        return remote(block_of(h, p, c), block_of(h, p, c), bs.at[h], br.at[h, o], at(q, c))

    def source(o):
        if o == PLANE - 1:
            return p
        dx, dy = PLANE_STEPS[o]
        return offset(x, y, -dx, -dy)

    def forward(h, o):
        return remote(block_of(h, source(o), c), block_of(h, source(o), c), fs.at[h], fr.at[h], sibling)

    for h in range(HALVES):
        for t in range(OWN_TILES):
            @pl.when(keeper(h, t) != z)
            def _(h=h, t=t):
                landed(tile_of(h, t), agr.at[h, t])
        for o in range(PLANE - 1):
            plane_out(h, o).start()
        forward(h, PLANE - 1).start()

    def image_part(h, core):
        total = None
        for j in range(NC):
            i = (NC if core is c else 0) + j
            block = sketch[h, :, :, lanes(core * OWN + j * WIDE, WIDE)]
            hi, lo = split2(block.reshape(HALF, WIDE))
            both = mm(jnp.concatenate([hi, lo], 0), emb_hi[i], NT)
            term = both[:HALF] + (both[HALF:] + mm(hi, emb_lo[i], NT))
            total = term if total is None else total + term
        return total

    halves = []
    for h in range(HALVES):
        for o in reversed(range(PLANE - 1)):
            block = block_of(h, source(o), c)
            landed(block, br.at[h, o])
            forward(h, o).start()
        halves.append(image_part(h, c))

    keeps_a = y % NC == c

    pairs = [(s, dc) for s in range(PLANE) for dc in range(NC) if (s, dc) != (0, 0)]

    def gram_a(s):
        q = offset(x, y, *around[s])
        slot = NC * s + ((q % NY) + c) % NC
        return remote(gram_part.at[0, q], gram_in_a.at[slot], gas.at[s], gar.at[0], at(q, (q % NY) % NC))

    def gram_b(s, dc):
        q, core = offset(x, y, *around[s]), (c + dc) % NC
        return remote(gram_part.at[1 + core, q], gram_in_b.at[NC * s + dc], gbs.at[0], gbr.at[0], at(q, core))

    pieces = []
    for h in range(HALVES):
        landed(part.at[h], fr.at[h])
        halves[h] = halves[h] + image_part(h, 1 - c)
        pieces += split2(halves[h])
        gram = mm(jnp.concatenate(pieces[-2:], 0), jnp.concatenate(pieces, 0), NT)
        gram = gram[:HALF] + gram[HALF:]
        for g in range(h + 1):
            block = gram[:, g * K:g * K + HALF] + gram[:, g * K + HALF:(g + 1) * K]
            gram_part[h + g] = block.reshape(PLANE, 8, 128)
        if h == 0:
            for s in range(1, PLANE):
                gram_a(s).start()

            @pl.when(jnp.logical_not(keeps_a))
            def _():
                gram_a(0).start()
        else:
            for s, dc in pairs:
                gram_b(s, dc).start()

    def gram_z_copy(store, send, recv, step):
        return remote(store.at[z], store.at[z], send.at[0], recv.at[0], device(x, (z + step) % NZ, y, c))

    @pl.when(keeps_a)
    def _():
        total = gram_part[0, p]
        landed(gram_in_a.at[pl.ds(1, 31)], gar.at[0])
        for slot in range(1, 32):
            total = total + gram_in_a[slot]
        gram_z_a[z] = total
        for step in Z_STEPS:
            gram_z_copy(gram_z_a, has, har, step).start()

    total = gram_part[1 + c, p]
    landed(gram_in_b.at[pl.ds(1, 31)], gbr.at[0])
    for slot in range(1, 32):
        total = total + gram_in_b[slot]
    gram_z_b[z] = total
    for step in Z_STEPS:
        gram_z_copy(gram_z_b, hbs, hbr, step).start()

    image[...] = jnp.concatenate(halves, 0).T
    image_copy = pltpu.make_async_copy(image, image_hbm, out_sem)
    image_copy.start()
    for h in range(HALVES):
        core_copy(h).wait_send()
        landed(plane_in.at[h], xs.at[h])
        landed(plane_in.at[h], bs.at[h])
        landed(part.at[h], fs.at[h])
        for t in range(OWN_TILES):
            @pl.when(keeper(h, t) != z)
            def _(h=h, t=t):
                z_copy(h, t).wait_send()

        @pl.when(keeps(h))
        def _():
            landed(z_in.at[pl.ds(1, NZ - 1)], ags.at[0])
    for s in range(1, PLANE):
        gram_a(s).wait_send()

    @pl.when(jnp.logical_not(keeps_a))
    def _():
        gram_a(0).wait_send()

    landed(gram_in_b.at[pl.ds(1, 31)], gbs.at[0])

    def z_sum(store, recv):
        landed(store.at[pl.ds(0, NZ - 1)], recv.at[0])
        total = store[0]
        for i in range(1, NZ):
            total = total + store[i]
        return total

    def gram_out_a(s, dc):
        block = gram_all.at[0, p]
        return remote(block, block, kas.at[0], kar.at[0], at(offset(x, y, *around[s]), (c + dc) % NC))

    def gram_out_b(s, dc):
        block = gram_all.at[1 + c, p]
        return remote(block, block, kbs.at[0], kbr.at[0], at(offset(x, y, *around[s]), (c + dc) % NC))

    @pl.when(keeps_a)
    def _():
        gram_all[0, p] = z_sum(gram_z_a, har)
        for s, dc in pairs:
            gram_out_a(s, dc).start()

    gram_all[1 + c, p] = z_sum(gram_z_b, hbr)
    for s, dc in pairs:
        gram_out_b(s, dc).start()

    @pl.when(keeps_a)
    def _():
        landed(gram_all.at[0, pl.ds(0, PLANE - 1)], kar.at[0])

    @pl.when(jnp.logical_not(keeps_a))
    def _():
        landed(gram_all.at[0], kar.at[0])

    first_ref[...] = first_inverse(gram_all[0].reshape(HALF, HALF))

    @pl.when(keeps_a)
    def _():
        landed(gram_z_a.at[pl.ds(0, NZ - 1)], has.at[0])
        landed(gram_in_a.at[pl.ds(1, 31)], kas.at[0])

    landed(gram_z_b.at[pl.ds(0, NZ - 1)], hbs.at[0])
    landed(gram_in_b.at[pl.ds(1, 31)], kbs.at[0])
    image_copy.wait()

    landed(gram_in_b.at[pl.ds(1, 31)], kbr.at[0])
    gram_ref[...] = gram_all[1:3].reshape(NC, HALF, HALF)


def sums(embeddings, start_basis):
    rows = embeddings.shape[0]
    dma = lambda *n: pltpu.SemaphoreType.DMA(n)
    vmem = pltpu.VMEM
    return pl.pallas_call(
        gather_kernel,
        out_shape=(
            jax.ShapeDtypeStruct((rows, K), F32),
            jax.ShapeDtypeStruct((NC, HALF, HALF), F32),
            jax.ShapeDtypeStruct((HALF, HALF), F32),
        ),
        in_specs=[pl.BlockSpec(memory_space=pl.ANY)] * 2,
        out_specs=(pl.BlockSpec(memory_space=pl.ANY),) + (pl.BlockSpec(memory_space=pltpu.VMEM),) * 2,
        scratch_shapes=[
            vmem((PARTS, rows, WIDE), F32),
            vmem((PARTS, rows, WIDE), BF16),
            vmem((PARTS, rows, WIDE), BF16),
            vmem((rows, K), F32),
            vmem((HALVES, PLANE, 8, OWN), F32),
            vmem((HALVES, PLANE, 8, OWN), F32),
            vmem((HALVES, PLANE, 8, OWN), F32),
            vmem((HALVES, PLANE - 1, 8, OWN), F32),
            vmem((HALVES, OWN_TILES, 8, 128), F32),
            vmem((NZ, 8, 128), F32),
            vmem((HALVES, PLANE, 8, D), F32),
            vmem((rows, K), F32),
            vmem((3, PLANE, 8, 128), F32),
            vmem((32, 8, 128), F32),
            vmem((32, 8, 128), F32),
            vmem((NZ, 8, 128), F32),
            vmem((NZ, 8, 128), F32),
            vmem((3, PLANE, 8, 128), F32),
            dma(PARTS + 1),
            dma(HALVES), dma(HALVES),
            dma(HALVES), dma(HALVES),
            dma(HALVES, OWN_TILES), dma(1),
            dma(1), dma(HALVES, OWN_TILES),
            dma(HALVES), dma(HALVES, PLANE),
            dma(HALVES), dma(HALVES),
            dma(PLANE), dma(1),
            dma(1), dma(1),
            dma(1), dma(1),
            dma(1), dma(1),
            dma(1), dma(1),
            dma(1), dma(1),
            pltpu.SemaphoreType.DMA,
            pltpu.SemaphoreType.REGULAR,
        ],
        compiler_params=pltpu.CompilerParams(
            collective_id=0, has_side_effects=True, vmem_limit_bytes=VMEM_BYTES
        ),
        name="sums",
    )(embeddings, start_basis)


LEFT = (0, 0, 1, 0, 2, 1)
RIGHT = (0, 1, 0, 2, 0, 1)


def stacked(pieces, order):
    return jnp.concatenate([pieces[i] for i in order], 0)


def spread(block, size):
    return [jnp.broadcast_to(block[:, j:j + 1], (size, 128)) for j in range(size)]


def eliminate(panels):
    size = BLOCK
    rows = lax.broadcasted_iota(jnp.int32, (size, 128), 0)
    done = []
    strips = [panel[:size] for panel in panels]
    rest = [panel[size:] for panel in panels]
    for off in range(0, HALF, size):
        last = off + size == HALF
        cols = spread(strips[0][:, off:off + size], size)
        if not last:
            ahead = spread(strips[0][:, off + size:off + 2 * size].T, size)
            change = [0.0] * len(strips)
        scale = jnp.zeros((size, 128), F32)
        for j in range(0, size, 2):
            cj, cn = cols[j], cols[j + 1]
            a, b, d = cj[j:j + 1], cj[j + 1:j + 2], cn[j + 1:j + 2]
            q = 1.0 / (a * d - b * b)
            aq, bq, dq = a * q, b * q, d * q
            u = cj * dq - cn * bq
            v = cn * aq - cj * bq
            for k in range(j + 2, size):
                lo = (k // 8) * 8
                new = cols[k][lo:] - (u[lo:] * cj[k:k + 1] + v[lo:] * cn[k:k + 1])
                cols[k] = jnp.concatenate([cols[k][:lo], new], 0) if lo else new
            if not last:
                aj, an = ahead[j], ahead[j + 1]
                au = aj * dq - an * bq
                av = an * aq - aj * bq
                for k in range(j + 2, size):
                    ahead[k] = ahead[k] - (au * cj[k:k + 1] + av * cn[k:k + 1])
                change = [t + (au * s[j:j + 1] + av * s[j + 1:j + 2]) for t, s in zip(change, strips)]
            below = rows > j + 1
            ba = b * (1.0 / a)
            um = jnp.where(below, u, jnp.where(rows == j + 1, ba, 0.0))
            vm = jnp.where(below, v, 0.0)
            strips = [s - (um * s[j:j + 1] + vm * s[j + 1:j + 2]) for s in strips]
            ra = lax.rsqrt(a)
            rd = lax.rsqrt(d - ba * b)
            scale = jnp.where(rows == j, ra, jnp.where(rows == j + 1, rd, scale))
        strips = [s * scale for s in strips]
        done.append(strips[1:])
        if last:
            break
        following = [r[:size] - t for r, t in zip(rest, change)]
        behind = off + 2 * size
        if behind < HALF:
            pieces = [split3(s) for s in strips]
            left = stacked(pieces[0], LEFT)
            right = jnp.concatenate([stacked(piece, RIGHT) for piece in pieces], 1)
            product = mm(left, right, TN)[behind:]
            rest = [r[size:] - product[:, 128 * i:128 * (i + 1)] for i, r in enumerate(rest)]
        strips = following
    return [jnp.concatenate([strips[i] for strips in done], 0) for i in range(len(panels) - 1)]


def mm6(a, b, dims):
    ah, am, al = split3(a)
    bh, bm, bl = split3(b)
    return mm(ah, bh, dims) + (mm(ah, bm, dims) + mm(am, bh, dims)) + (mm(am, bm, dims) + (mm(ah, bl, dims) + mm(al, bh, dims)))


def diagonal():
    return lax.broadcasted_iota(jnp.int32, (HALF, HALF), 0) == lax.broadcasted_iota(jnp.int32, (HALF, HALF), 1)


def diagonal_scales(value):
    entries = jnp.where(diagonal(), value, 0.0)
    return (
        lax.rsqrt(jnp.sum(entries, axis=1, keepdims=True)),
        lax.rsqrt(jnp.sum(entries, axis=0, keepdims=True)),
    )


def first_inverse(aa):
    col, row = diagonal_scales(aa)
    (inverse,) = eliminate([aa * col * row, jnp.where(diagonal(), 1.0, 0.0)])
    return inverse * row


def basis_kernel(scale, gram_ref, first_ref, image_hbm, out_hbm, image, out, sems):
    copy = pltpu.make_async_copy(image_hbm, image, sems.at[0])
    copy.start()
    first = first_ref[...]
    ba, bb = gram_ref[0], gram_ref[1]
    col, row = diagonal_scales(bb)
    cross = mm6(ba * col, first, NT)
    rest = bb * col * row - mm6(cross, cross, NT)
    lower = mm6(cross, first, NN)
    copy.wait()
    rows = image.shape[0]
    outs = []

    def product(value, factor):
        hi, lo = split2(value)
        high, low = split2(factor)
        both = mm(hi, jnp.concatenate([high, low], 0), NT)
        return both[:, :HALF] + (both[:, HALF:] + mm(lo, high, NT))

    def leave(r, n, cols):
        outs.append(pltpu.make_async_copy(out.at[pl.ds(r, n), cols], out_hbm.at[pl.ds(r, n), cols], sems.at[1 + len(outs)]))
        outs[-1].start()

    out[:, :HALF] = product(image[:, :HALF], first * scale)
    leave(0, rows, pl.ds(0, HALF))
    below, second = eliminate([rest, -lower, jnp.where(diagonal(), 1.0, 0.0)])
    factor = jnp.concatenate([below, second * row], 1) * scale
    step = rows // 2
    for r in range(0, rows, step):
        out[r:r + step, HALF:] = product(image[r:r + step, :], factor)
        leave(r, step, pl.ds(HALF, HALF))
    for copy in outs:
        copy.wait()


def basis_of(gram, first, image, scale):
    rows = image.shape[0]
    in_vmem = pl.BlockSpec(memory_space=pltpu.VMEM)
    return pl.pallas_call(
        functools.partial(basis_kernel, scale),
        out_shape=jax.ShapeDtypeStruct((rows, K), F32),
        in_specs=[in_vmem, in_vmem, pl.BlockSpec(memory_space=pl.ANY)],
        out_specs=pl.BlockSpec(memory_space=pl.ANY),
        scratch_shapes=[pltpu.VMEM((rows, K), F32), pltpu.VMEM((rows, K), F32), pltpu.SemaphoreType.DMA((4,))],
        compiler_params=pltpu.CompilerParams(vmem_limit_bytes=VMEM_BYTES),
        name="basis",
    )(gram, first, image)


def local(embeddings, start_basis):
    total_rows = embeddings.shape[0] * lax.axis_size("dp")
    image, gram, first = sums(embeddings, start_basis)
    return basis_of(gram, first, image, float(total_rows) ** 0.5)


def solution(mesh):
    in_specs = (P("dp", None), P("dp", None))
    out_specs = P("dp", None)
    return jax.shard_map(local, mesh=mesh, in_specs=in_specs, out_specs=out_specs, check_vma=False)
```

```python
import functools

import jax
import jax.numpy as jnp
from jax import lax
from jax.experimental import pallas as pl
from jax.experimental.pallas import tpu as pltpu
from jax.sharding import PartitionSpec as P

F32, BF16 = jnp.float32, jnp.bfloat16
NX, NZ, NY, NC = 4, 16, 4, 2
PLANE = NX * NY
D, K = 1024, 256
PARTS = 4
WIDE = D // PARTS
HALVES = 2
HALF = K // HALVES
OWN = D // NC
OWN_TILES = OWN // 128
BLOCK = 16
VMEM_BYTES = 60 << 20

PLANE_STEPS = sorted(
    [(dx, dy) for dx in range(NX) for dy in range(NY) if (dx, dy) != (0, 0)],
    key=lambda s: -(min(s[0], NX - s[0]) + min(s[1], NY - s[1])),
)
PLANE_CORE_STEPS = [(dx, dy, dc) for dx, dy in PLANE_STEPS for dc in range(NC)] + [(0, 0, 1)]
Z_STEPS = sorted(range(1, NZ), key=lambda d: -min(d, NZ - d))

NT = (((1,), (1,)), ((), ()))
NN = (((1,), (0,)), ((), ()))
TN = (((0,), (0,)), ((), ()))


def mm(a, b, dims):
    return lax.dot_general(a, b, dims, preferred_element_type=F32)


def split2(value):
    high = value.astype(BF16)
    return high, (value - high.astype(F32)).astype(BF16)


def split3(value):
    high = value.astype(BF16)
    rest = value - high.astype(F32)
    middle = rest.astype(BF16)
    return high, middle, (rest - middle.astype(F32)).astype(BF16)


def device(x, z, y, c):
    return ((x * NZ + z) * NY + y) * NC + c


def remote(src, dst, send, recv, target):
    return pltpu.make_async_remote_copy(
        src_ref=src,
        dst_ref=dst,
        send_sem=send,
        recv_sem=recv,
        device_id={"dp": target},
        device_id_type=pl.DeviceIdType.MESH,
    )


def mod(value, n):
    return lax.rem(value, n)


def offset(x, y, dx, dy):
    return mod(x + dx % NX, NX) * NY + mod(y + dy % NY, NY)


def landed(ref, sem):
    pltpu.make_async_copy(ref, ref, sem).wait()


def gather_kernel(
    emb_hbm, start_hbm, image_hbm, gram_hbm, first_hbm,
    emb, emb_hi, emb_lo, start, give, core_in, part, plane_in, tiles, z_in, sketch,
    image, gram_part, gram_in_a, gram_in_b, gram_z_a, gram_z_b, gram_a_all, gram_b_own, first,
    load_sem, core_s, core_r, xs, xr, zs, zr, ags, agr, bs, br, fs, fr,
    gas, gar, gbs, gbr, has, har, hbs, hbr, kas, kar, kbs, kbr, out_sem, relay,
):
    me = lax.axis_index("dp")
    x, z, y, c = lax.div(me, NZ * NY * NC), mod(lax.div(me, NY * NC), NZ), mod(lax.div(me, NC), NY), mod(me, NC)
    p = x * NY + y
    sibling = device(x, z, y, 1 - c)
    around = [(0, 0)] + PLANE_STEPS

    def at(q, core):
        return device(lax.div(q, NY), z, mod(q, NY), core)

    places = [NC * (1 - c), NC * (1 - c) + 1, NC * c, NC * c + 1]

    def wide(i):
        return pl.ds(pl.multiple_of(places[i] * WIDE, WIDE), WIDE)

    loads = [pltpu.make_async_copy(start_hbm, start, load_sem.at[PARTS])]
    loads += [pltpu.make_async_copy(emb_hbm.at[:, wide(i)], emb.at[i], load_sem.at[i]) for i in range(PARTS)]
    for copy in loads:
        copy.start()

    barrier = pltpu.get_barrier_semaphore()
    greeted = [device(x, mod(z + step, NZ), y, c) for step in Z_STEPS if min(step, NZ - step) <= NZ // 4]
    greeted += [at(offset(x, y, dx, dy), mod(c + dc, NC)) for dx, dy, dc in PLANE_CORE_STEPS]
    for other in greeted:
        pl.semaphore_signal(barrier, inc=1, device_id={"dp": other}, device_id_type=pl.DeviceIdType.MESH)

    loads[0].wait()
    start_hi, start_lo = split2(start[...].T)

    def core_copy(h):
        return remote(give.at[h], core_in.at[h], core_s.at[h], core_r.at[h], sibling)

    for i in range(PARTS):
        if i == NC:
            pl.semaphore_wait(barrier, len(greeted))
            for h in range(HALVES):
                core_copy(h).start()
        loads[1 + i].wait()
        hi, lo = split2(emb[i])
        emb_hi[i] = hi
        emb_lo[i] = lo
        total = mm(start_hi, hi, NN) + (mm(start_hi, lo, NN) + mm(start_lo, hi, NN))
        store, j = (give, i) if i < NC else (part, i - NC)
        store[:, :, :, j * WIDE:(j + 1) * WIDE] = total.reshape(HALVES, PLANE, 8, WIDE)

    for step in (NZ // 4, NZ - NZ // 4):
        pl.semaphore_signal(relay, inc=1, device_id={"dp": device(x, mod(z + step, NZ), y, c)}, device_id_type=pl.DeviceIdType.MESH)

    def plane_copy(h, o):
        q = offset(x, y, *PLANE_STEPS[o])
        return remote(part.at[h, q], plane_in.at[h, o], xs.at[h], xr.at[h], at(q, c))

    for h in range(HALVES):
        core_copy(h).wait_recv()
        part[h] = part[h] + core_in[h]
        for o in range(PLANE - 1):
            plane_copy(h, o).start()

    pl.semaphore_wait(relay, 2)

    def keeper(h, t):
        return 4 * t + NC * h + c

    def z_copy(h, t):
        step = mod(keeper(h, t) - z + NZ, NZ)
        return remote(tiles.at[h, t], z_in.at[step], zs.at[h, t], zr.at[0], device(x, keeper(h, t), y, c))

    for h in range(HALVES):
        landed(plane_in.at[h], xr.at[h])
        total = part[h, p]
        for o in range(PLANE - 1):
            total = total + plane_in[h, o]
        for t in range(OWN_TILES):
            tiles[h, t] = total[:, t * 128:(t + 1) * 128]
        for t in range(OWN_TILES):
            @pl.when(keeper(h, t) != z)
            def _(h=h, t=t):
                z_copy(h, t).start()

    def lanes(start, size):
        return pl.ds(pl.multiple_of(start, 128), size)

    def tile_of(h, t):
        return sketch.at[h, p, :, lanes(c * OWN + t * 128, 128)]

    mine = lax.div(z, 4)

    def z_out(h, step):
        return remote(tile_of(h, mine), tile_of(h, mine), ags.at[0], agr.at[h, mine], device(x, mod(z + step, NZ), y, c))

    def keeps(h):
        return mod(z, 4) == NC * h + c

    for h in range(HALVES):
        @pl.when(keeps(h))
        def _(h=h):
            landed(z_in.at[pl.ds(1, NZ - 1)], zr.at[0])
            total = tiles[h, mine]
            for step in range(1, NZ):
                total = total + z_in[step]
            sketch[h, p, :, lanes(c * OWN + mine * 128, 128)] = total
            for step in Z_STEPS:
                z_out(h, step).start()

    def block_of(h, q, core):
        return sketch.at[h, q, :, lanes(core * OWN, OWN)]

    def plane_out(h, o):
        q = offset(x, y, *PLANE_STEPS[o])
        return remote(block_of(h, p, c), block_of(h, p, c), bs.at[h], br.at[h, o], at(q, c))

    def source(o):
        if o == PLANE - 1:
            return p
        dx, dy = PLANE_STEPS[o]
        return offset(x, y, -dx, -dy)

    def forward(h, o):
        return remote(block_of(h, source(o), c), block_of(h, source(o), c), fs.at[h], fr.at[h], sibling)

    for h in range(HALVES):
        for t in range(OWN_TILES):
            @pl.when(keeper(h, t) != z)
            def _(h=h, t=t):
                landed(tile_of(h, t), agr.at[h, t])
        for o in range(PLANE - 1):
            plane_out(h, o).start()
        forward(h, PLANE - 1).start()

    def image_part(h, core):
        total = None
        for j in range(NC):
            i = (NC if core is c else 0) + j
            block = sketch[h, :, :, lanes(core * OWN + j * WIDE, WIDE)]
            hi, lo = split2(block.reshape(HALF, WIDE))
            both = mm(jnp.concatenate([hi, lo], 0), emb_hi[i], NT)
            term = both[:HALF] + (both[HALF:] + mm(hi, emb_lo[i], NT))
            total = term if total is None else total + term
        return total

    halves = []
    for h in range(HALVES):
        for o in reversed(range(PLANE - 1)):
            block = block_of(h, source(o), c)
            landed(block, br.at[h, o])
            forward(h, o).start()
        halves.append(image_part(h, c))

    keeps_a = mod(y, NC) == c

    pairs = [(s, dc) for s in range(PLANE) for dc in range(NC) if (s, dc) != (0, 0)]

    def gram_a(s):
        q = offset(x, y, *around[s])
        slot = NC * s + mod(q + c, NC)
        return remote(gram_part.at[0, q], gram_in_a.at[slot], gas.at[s], gar.at[0], at(q, mod(q, NC)))

    def gram_b(s, dc):
        q, core = offset(x, y, *around[s]), mod(c + dc, NC)
        return remote(gram_part.at[1 + core, q], gram_in_b.at[NC * s + dc], gbs.at[0], gbr.at[0], at(q, core))

    pieces = []
    for h in range(HALVES):
        landed(part.at[h], fr.at[h])
        halves[h] = halves[h] + image_part(h, 1 - c)
        pieces += split2(halves[h])
        gram = mm(jnp.concatenate(pieces[-2:], 0), jnp.concatenate(pieces, 0), NT)
        gram = gram[:HALF] + gram[HALF:]
        for g in range(h + 1):
            block = gram[:, g * K:g * K + HALF] + gram[:, g * K + HALF:(g + 1) * K]
            gram_part[h + g] = block.reshape(PLANE, 8, 128)
        if h == 0:
            for s in range(1, PLANE):
                gram_a(s).start()

            @pl.when(jnp.logical_not(keeps_a))
            def _():
                gram_a(0).start()
        else:
            for s, dc in pairs:
                gram_b(s, dc).start()

    def gram_z_copy(store, send, recv, step):
        return remote(store.at[z], store.at[z], send.at[0], recv.at[0], device(x, mod(z + step, NZ), y, c))

    @pl.when(keeps_a)
    def _():
        total = gram_part[0, p]
        landed(gram_in_a.at[pl.ds(1, 31)], gar.at[0])
        for slot in range(1, 32):
            total = total + gram_in_a[slot]
        gram_z_a[z] = total
        for step in Z_STEPS:
            gram_z_copy(gram_z_a, has, har, step).start()

    total = gram_part[1 + c, p]
    landed(gram_in_b.at[pl.ds(1, 31)], gbr.at[0])
    for slot in range(1, 32):
        total = total + gram_in_b[slot]
    gram_z_b[z] = total
    for step in Z_STEPS:
        gram_z_copy(gram_z_b, hbs, hbr, step).start()

    image[...] = jnp.concatenate(halves, 0).T
    image_copy = pltpu.make_async_copy(image, image_hbm, out_sem.at[0])
    image_copy.start()
    for h in range(HALVES):
        core_copy(h).wait_send()
        landed(plane_in.at[h], xs.at[h])
        landed(plane_in.at[h], bs.at[h])
        landed(part.at[h], fs.at[h])
        for t in range(OWN_TILES):
            @pl.when(keeper(h, t) != z)
            def _(h=h, t=t):
                z_copy(h, t).wait_send()

        @pl.when(keeps(h))
        def _():
            landed(z_in.at[pl.ds(1, NZ - 1)], ags.at[0])
    for s in range(1, PLANE):
        gram_a(s).wait_send()

    @pl.when(jnp.logical_not(keeps_a))
    def _():
        gram_a(0).wait_send()

    landed(gram_in_b.at[pl.ds(1, 31)], gbs.at[0])

    def z_sum(store, recv):
        landed(store.at[pl.ds(0, NZ - 1)], recv.at[0])
        total = store[0]
        for i in range(1, NZ):
            total = total + store[i]
        return total

    def gram_out_a(s, dc):
        block = gram_a_all.at[p]
        return remote(block, block, kas.at[0], kar.at[0], at(offset(x, y, *around[s]), mod(c + dc, NC)))

    def gram_out_b(s, dc):
        other = at(offset(x, y, *around[s]), mod(c + dc, NC))
        return remote(gram_b_own, gram_hbm.at[c, p], kbs.at[0], kbr.at[0], other)

    @pl.when(keeps_a)
    def _():
        gram_a_all[p] = z_sum(gram_z_a, har)
        for s, dc in pairs:
            gram_out_a(s, dc).start()

    gram_b_own[...] = z_sum(gram_z_b, hbr)
    for s, dc in pairs:
        gram_out_b(s, dc).start()
    own_copy = pltpu.make_async_copy(gram_b_own, gram_hbm.at[c, p], out_sem.at[1])
    own_copy.start()

    @pl.when(keeps_a)
    def _():
        landed(gram_a_all.at[pl.ds(0, PLANE - 1)], kar.at[0])

    @pl.when(jnp.logical_not(keeps_a))
    def _():
        landed(gram_a_all, kar.at[0])

    first[...] = first_inverse(gram_a_all[...].reshape(HALF, HALF))
    first_copy = pltpu.make_async_copy(first, first_hbm, out_sem.at[2])
    first_copy.start()

    @pl.when(keeps_a)
    def _():
        landed(gram_z_a.at[pl.ds(0, NZ - 1)], has.at[0])
        landed(gram_in_a.at[pl.ds(1, 31)], kas.at[0])

    landed(gram_z_b.at[pl.ds(0, NZ - 1)], hbs.at[0])
    landed(gram_in_b.at[pl.ds(1, 31)], kbs.at[0])
    image_copy.wait()
    own_copy.wait()
    first_copy.wait()

    landed(gram_in_b.at[pl.ds(1, 31)], kbr.at[0])


def sums(embeddings, start_basis):
    rows = embeddings.shape[0]
    dma = lambda *n: pltpu.SemaphoreType.DMA(n)
    vmem = pltpu.VMEM
    return pl.pallas_call(
        gather_kernel,
        out_shape=(
            jax.ShapeDtypeStruct((rows, K), F32),
            jax.ShapeDtypeStruct((NC, PLANE, 8, 128), F32),
            jax.ShapeDtypeStruct((HALF, HALF), F32),
        ),
        in_specs=[pl.BlockSpec(memory_space=pl.ANY)] * 2,
        out_specs=(pl.BlockSpec(memory_space=pl.ANY),) * 3,
        scratch_shapes=[
            vmem((PARTS, rows, WIDE), F32),
            vmem((PARTS, rows, WIDE), BF16),
            vmem((PARTS, rows, WIDE), BF16),
            vmem((rows, K), F32),
            vmem((HALVES, PLANE, 8, OWN), F32),
            vmem((HALVES, PLANE, 8, OWN), F32),
            vmem((HALVES, PLANE, 8, OWN), F32),
            vmem((HALVES, PLANE - 1, 8, OWN), F32),
            vmem((HALVES, OWN_TILES, 8, 128), F32),
            vmem((NZ, 8, 128), F32),
            vmem((HALVES, PLANE, 8, D), F32),
            vmem((rows, K), F32),
            vmem((3, PLANE, 8, 128), F32),
            vmem((32, 8, 128), F32),
            vmem((32, 8, 128), F32),
            vmem((NZ, 8, 128), F32),
            vmem((NZ, 8, 128), F32),
            vmem((PLANE, 8, 128), F32),
            vmem((8, 128), F32),
            vmem((HALF, HALF), F32),
            dma(PARTS + 1),
            dma(HALVES), dma(HALVES),
            dma(HALVES), dma(HALVES),
            dma(HALVES, OWN_TILES), dma(1),
            dma(1), dma(HALVES, OWN_TILES),
            dma(HALVES), dma(HALVES, PLANE),
            dma(HALVES), dma(HALVES),
            dma(PLANE), dma(1),
            dma(1), dma(1),
            dma(1), dma(1),
            dma(1), dma(1),
            dma(1), dma(1),
            dma(1), dma(1),
            dma(3),
            pltpu.SemaphoreType.REGULAR,
        ],
        compiler_params=pltpu.CompilerParams(
            collective_id=0, has_side_effects=True, vmem_limit_bytes=VMEM_BYTES
        ),
        name="sums",
    )(embeddings, start_basis)


LEFT = (0, 0, 1, 0, 2, 1)
RIGHT = (0, 1, 0, 2, 0, 1)


def stacked(pieces, order):
    return jnp.concatenate([pieces[i] for i in order], 0)


def spread(block, size):
    return [jnp.broadcast_to(block[:, j:j + 1], (size, 128)) for j in range(size)]


def eliminate(panels):
    size = BLOCK
    rows = lax.broadcasted_iota(jnp.int32, (size, 128), 0)
    done = []
    strips = [panel[:size] for panel in panels]
    rest = [panel[size:] for panel in panels]
    for off in range(0, HALF, size):
        last = off + size == HALF
        cols = spread(strips[0][:, off:off + size], size)
        if not last:
            ahead = spread(strips[0][:, off + size:off + 2 * size].T, size)
            change = [0.0] * len(strips)
        scale = jnp.zeros((size, 128), F32)
        for j in range(0, size, 2):
            cj, cn = cols[j], cols[j + 1]
            a, b, d = cj[j:j + 1], cj[j + 1:j + 2], cn[j + 1:j + 2]
            q = 1.0 / (a * d - b * b)
            aq, bq, dq = a * q, b * q, d * q
            u = cj * dq - cn * bq
            v = cn * aq - cj * bq
            for k in range(j + 2, size):
                lo = (k // 8) * 8
                new = cols[k][lo:] - (u[lo:] * cj[k:k + 1] + v[lo:] * cn[k:k + 1])
                cols[k] = jnp.concatenate([cols[k][:lo], new], 0) if lo else new
            if not last:
                aj, an = ahead[j], ahead[j + 1]
                au = aj * dq - an * bq
                av = an * aq - aj * bq
                for k in range(j + 2, size):
                    ahead[k] = ahead[k] - (au * cj[k:k + 1] + av * cn[k:k + 1])
                change = [t + (au * s[j:j + 1] + av * s[j + 1:j + 2]) for t, s in zip(change, strips)]
            below = rows > j + 1
            ba = b * (1.0 / a)
            um = jnp.where(below, u, jnp.where(rows == j + 1, ba, 0.0))
            vm = jnp.where(below, v, 0.0)
            strips = [s - (um * s[j:j + 1] + vm * s[j + 1:j + 2]) for s in strips]
            ra = lax.rsqrt(a)
            rd = lax.rsqrt(d - ba * b)
            scale = jnp.where(rows == j, ra, jnp.where(rows == j + 1, rd, scale))
        strips = [s * scale for s in strips]
        done.append(strips[1:])
        if last:
            break
        following = [r[:size] - t for r, t in zip(rest, change)]
        behind = off + 2 * size
        if behind < HALF:
            pieces = [split3(s) for s in strips]
            left = stacked(pieces[0], LEFT)
            right = jnp.concatenate([stacked(piece, RIGHT) for piece in pieces], 1)
            product = mm(left, right, TN)[behind:]
            rest = [r[size:] - product[:, 128 * i:128 * (i + 1)] for i, r in enumerate(rest)]
        strips = following
    return [jnp.concatenate([strips[i] for strips in done], 0) for i in range(len(panels) - 1)]


def mm6(a, b, dims):
    ah, am, al = split3(a)
    bh, bm, bl = split3(b)
    return mm(ah, bh, dims) + (mm(ah, bm, dims) + mm(am, bh, dims)) + (mm(am, bm, dims) + (mm(ah, bl, dims) + mm(al, bh, dims)))


def diagonal():
    return lax.broadcasted_iota(jnp.int32, (HALF, HALF), 0) == lax.broadcasted_iota(jnp.int32, (HALF, HALF), 1)


def diagonal_scales(value):
    entries = jnp.where(diagonal(), value, 0.0)
    return (
        lax.rsqrt(jnp.sum(entries, axis=1, keepdims=True)),
        lax.rsqrt(jnp.sum(entries, axis=0, keepdims=True)),
    )


def first_inverse(aa):
    col, row = diagonal_scales(aa)
    (inverse,) = eliminate([aa * col * row, jnp.where(diagonal(), 1.0, 0.0)])
    return inverse * row


def basis_kernel(scale, gram_hbm, first_hbm, image_hbm, out_hbm, gram, first_in, image, out, sems):
    loads = [
        pltpu.make_async_copy(src, dst, sems.at[i])
        for i, (src, dst) in enumerate([(gram_hbm, gram), (first_hbm, first_in), (image_hbm, image)])
    ]
    for copy in loads:
        copy.start()
    loads[0].wait()
    ba, bb = gram[0].reshape(HALF, HALF), gram[1].reshape(HALF, HALF)
    col, row = diagonal_scales(bb)
    loads[1].wait()
    first = first_in[...]
    cross = mm6(ba * col, first, NT)
    rest = bb * col * row - mm6(cross, cross, NT)
    lower = mm6(cross, first, NN)
    loads[2].wait()
    rows = image.shape[0]
    outs = []

    def product(value, factor):
        hi, lo = split2(value)
        high, low = split2(factor)
        both = mm(hi, jnp.concatenate([high, low], 0), NT)
        return both[:, :HALF] + (both[:, HALF:] + mm(lo, high, NT))

    def leave(r, n, cols):
        outs.append(pltpu.make_async_copy(out.at[pl.ds(r, n), cols], out_hbm.at[pl.ds(r, n), cols], sems.at[3 + len(outs)]))
        outs[-1].start()

    out[:, :HALF] = product(image[:, :HALF], first * scale)
    leave(0, rows, pl.ds(0, HALF))
    below, second = eliminate([rest, -lower, jnp.where(diagonal(), 1.0, 0.0)])
    factor = jnp.concatenate([below, second * row], 1) * scale
    step = rows // 2
    for r in range(0, rows, step):
        out[r:r + step, HALF:] = product(image[r:r + step, :], factor)
        leave(r, step, pl.ds(HALF, HALF))
    for copy in outs:
        copy.wait()


def basis_of(gram, first, image, scale):
    rows = image.shape[0]
    return pl.pallas_call(
        functools.partial(basis_kernel, scale),
        out_shape=jax.ShapeDtypeStruct((rows, K), F32),
        in_specs=[pl.BlockSpec(memory_space=pl.ANY)] * 3,
        out_specs=pl.BlockSpec(memory_space=pl.ANY),
        scratch_shapes=[
            pltpu.VMEM((NC, PLANE, 8, 128), F32),
            pltpu.VMEM((HALF, HALF), F32),
            pltpu.VMEM((rows, K), F32),
            pltpu.VMEM((rows, K), F32),
            pltpu.SemaphoreType.DMA((6,)),
        ],
        compiler_params=pltpu.CompilerParams(vmem_limit_bytes=VMEM_BYTES),
        name="basis",
    )(gram, first, image)


def local(embeddings, start_basis):
    total_rows = embeddings.shape[0] * lax.axis_size("dp")
    image, gram, first = sums(embeddings, start_basis)
    return basis_of(gram, first, image, float(total_rows) ** 0.5)


def solution(mesh):
    in_specs = (P("dp", None), P("dp", None))
    out_specs = P("dp", None)
    return jax.shard_map(local, mesh=mesh, in_specs=in_specs, out_specs=out_specs, check_vma=False)
```

```python
import functools

import jax
import jax.numpy as jnp
from jax import lax
from jax.experimental import pallas as pl
from jax.experimental.pallas import tpu as pltpu
from jax.sharding import PartitionSpec as P

F32, BF16 = jnp.float32, jnp.bfloat16
NX, NZ, NY, NC = 4, 16, 4, 2
PLANE = NX * NY
D, K = 1024, 256
PARTS = 4
WIDE = D // PARTS
HALVES = 2
HALF = K // HALVES
OWN = D // NC
OWN_TILES = OWN // 128
BLOCK = 16
VMEM_BYTES = 60 << 20

PLANE_STEPS = sorted(
    [(dx, dy) for dx in range(NX) for dy in range(NY) if (dx, dy) != (0, 0)],
    key=lambda s: -(min(s[0], NX - s[0]) + min(s[1], NY - s[1])),
)
PLANE_CORE_STEPS = [(dx, dy, dc) for dx, dy in PLANE_STEPS for dc in range(NC)] + [(0, 0, 1)]
Z_STEPS = sorted(range(1, NZ), key=lambda d: -min(d, NZ - d))

NT = (((1,), (1,)), ((), ()))
NN = (((1,), (0,)), ((), ()))
TN = (((0,), (0,)), ((), ()))


def mm(a, b, dims):
    return lax.dot_general(a, b, dims, preferred_element_type=F32)


def split2(value):
    high = value.astype(BF16)
    return high, (value - high.astype(F32)).astype(BF16)


def split3(value):
    high = value.astype(BF16)
    rest = value - high.astype(F32)
    middle = rest.astype(BF16)
    return high, middle, (rest - middle.astype(F32)).astype(BF16)


def device(x, z, y, c):
    return ((x * NZ + z) * NY + y) * NC + c


def remote(src, dst, send, recv, target):
    return pltpu.make_async_remote_copy(
        src_ref=src,
        dst_ref=dst,
        send_sem=send,
        recv_sem=recv,
        device_id={"dp": target},
        device_id_type=pl.DeviceIdType.MESH,
    )


def mod(value, n):
    return lax.rem(value, n)


def offset(x, y, dx, dy):
    return mod(x + dx % NX, NX) * NY + mod(y + dy % NY, NY)


def landed(ref, sem):
    pltpu.make_async_copy(ref, ref, sem).wait()


def gather_kernel(
    emb_hbm, start_hbm, image_hbm, gram_hbm, first_hbm,
    emb, emb_hi, emb_lo, start, give, core_in, part, plane_in, tiles, z_in, sketch,
    image, gram_part, gram_in_a, gram_in_b, gram_z_a, gram_z_b, gram_a_all, gram_b_own, first,
    load_sem, core_s, core_r, xs, xr, zs, zr, ags, agr, bs, br, fs, fr,
    gas, gar, gbs, gbr, has, har, hbs, hbr, kas, kar, kbs, kbr, out_sem, relay,
):
    me = lax.axis_index("dp")
    x, z, y, c = lax.div(me, NZ * NY * NC), mod(lax.div(me, NY * NC), NZ), mod(lax.div(me, NC), NY), mod(me, NC)
    p = x * NY + y
    sibling = device(x, z, y, 1 - c)
    around = [(0, 0)] + PLANE_STEPS

    def at(q, core):
        return device(lax.div(q, NY), z, mod(q, NY), core)

    places = [NC * (1 - c), NC * (1 - c) + 1, NC * c, NC * c + 1]

    def wide(i):
        return pl.ds(pl.multiple_of(places[i] * WIDE, WIDE), WIDE)

    loads = [pltpu.make_async_copy(start_hbm, start, load_sem.at[PARTS])]
    loads += [pltpu.make_async_copy(emb_hbm.at[:, wide(i)], emb.at[i], load_sem.at[i]) for i in range(PARTS)]
    for copy in loads:
        copy.start()

    barrier = pltpu.get_barrier_semaphore()
    greeted = [device(x, mod(z + step, NZ), y, c) for step in Z_STEPS if min(step, NZ - step) <= NZ // 4]
    greeted += [at(offset(x, y, dx, dy), mod(c + dc, NC)) for dx, dy, dc in PLANE_CORE_STEPS]
    for other in greeted:
        pl.semaphore_signal(barrier, inc=1, device_id={"dp": other}, device_id_type=pl.DeviceIdType.MESH)

    loads[0].wait()
    start_hi, start_lo = split2(start[...].T)

    def core_copy(h):
        return remote(give.at[h], core_in.at[h], core_s.at[h], core_r.at[h], sibling)

    for i in range(PARTS):
        if i == NC:
            pl.semaphore_wait(barrier, len(greeted))
            for h in range(HALVES):
                core_copy(h).start()
        loads[1 + i].wait()
        hi, lo = split2(emb[i])
        emb_hi[i] = hi
        emb_lo[i] = lo
        total = mm(start_hi, hi, NN) + (mm(start_hi, lo, NN) + mm(start_lo, hi, NN))
        store, j = (give, i) if i < NC else (part, i - NC)
        store[:, :, :, j * WIDE:(j + 1) * WIDE] = total.reshape(HALVES, PLANE, 8, WIDE)

    for step in (NZ // 4, NZ - NZ // 4):
        pl.semaphore_signal(relay, inc=1, device_id={"dp": device(x, mod(z + step, NZ), y, c)}, device_id_type=pl.DeviceIdType.MESH)

    def plane_copy(h, o):
        q = offset(x, y, *PLANE_STEPS[o])
        return remote(part.at[h, q], plane_in.at[h, o], xs.at[h], xr.at[h], at(q, c))

    for h in range(HALVES):
        core_copy(h).wait_recv()
        part[h] = part[h] + core_in[h]
        for o in range(PLANE - 1):
            plane_copy(h, o).start()

    pl.semaphore_wait(relay, 2)

    def keeper(h, t):
        return 4 * t + NC * h + c

    def z_copy(h, t):
        step = mod(keeper(h, t) - z + NZ, NZ)
        return remote(tiles.at[h, t], z_in.at[step], zs.at[h, t], zr.at[0], device(x, keeper(h, t), y, c))

    for h in range(HALVES):
        landed(plane_in.at[h], xr.at[h])
        total = part[h, p]
        for o in range(PLANE - 1):
            total = total + plane_in[h, o]
        for t in range(OWN_TILES):
            tiles[h, t] = total[:, t * 128:(t + 1) * 128]
        for t in range(OWN_TILES):
            @pl.when(keeper(h, t) != z)
            def _(h=h, t=t):
                z_copy(h, t).start()

    def lanes(start, size):
        return pl.ds(pl.multiple_of(start, 128), size)

    def tile_of(h, t):
        return sketch.at[h, p, :, lanes(c * OWN + t * 128, 128)]

    mine = lax.div(z, 4)

    def z_out(h, step):
        return remote(tile_of(h, mine), tile_of(h, mine), ags.at[0], agr.at[h, mine], device(x, mod(z + step, NZ), y, c))

    def keeps(h):
        return mod(z, 4) == NC * h + c

    for h in range(HALVES):
        @pl.when(keeps(h))
        def _(h=h):
            landed(z_in.at[pl.ds(1, NZ - 1)], zr.at[0])
            total = tiles[h, mine]
            for step in range(1, NZ):
                total = total + z_in[step]
            sketch[h, p, :, lanes(c * OWN + mine * 128, 128)] = total
            for step in Z_STEPS:
                z_out(h, step).start()

    def block_of(h, q, core):
        return sketch.at[h, q, :, lanes(core * OWN, OWN)]

    def plane_out(h, o):
        q = offset(x, y, *PLANE_STEPS[o])
        return remote(block_of(h, p, c), block_of(h, p, c), bs.at[h], br.at[h, o], at(q, c))

    def source(o):
        if o == PLANE - 1:
            return p
        dx, dy = PLANE_STEPS[o]
        return offset(x, y, -dx, -dy)

    def forward(h, o):
        return remote(block_of(h, source(o), c), block_of(h, source(o), c), fs.at[h], fr.at[h], sibling)

    for h in range(HALVES):
        for t in range(OWN_TILES):
            @pl.when(keeper(h, t) != z)
            def _(h=h, t=t):
                landed(tile_of(h, t), agr.at[h, t])
        for o in range(PLANE - 1):
            plane_out(h, o).start()
        forward(h, PLANE - 1).start()

    def image_part(h, core):
        total = None
        for j in range(NC):
            i = (NC if core is c else 0) + j
            block = sketch[h, :, :, lanes(core * OWN + j * WIDE, WIDE)]
            hi, lo = split2(block.reshape(HALF, WIDE))
            both = mm(jnp.concatenate([hi, lo], 0), emb_hi[i], NT)
            term = both[:HALF] + (both[HALF:] + mm(hi, emb_lo[i], NT))
            total = term if total is None else total + term
        return total

    halves = []
    for h in range(HALVES):
        for o in reversed(range(PLANE - 1)):
            block = block_of(h, source(o), c)
            landed(block, br.at[h, o])
            forward(h, o).start()
        if h == 0:
            halves.append(image_part(h, c))

    keeps_a = mod(y, NC) == c

    pairs = [(s, dc) for s in range(PLANE) for dc in range(NC) if (s, dc) != (0, 0)]

    def gram_a(s):
        q = offset(x, y, *around[s])
        slot = NC * s + mod(q + c, NC)
        return remote(gram_part.at[0, q], gram_in_a.at[slot], gas.at[s], gar.at[0], at(q, mod(q, NC)))

    def gram_b(s, dc):
        q, core = offset(x, y, *around[s]), mod(c + dc, NC)
        return remote(gram_part.at[1 + core, q], gram_in_b.at[NC * s + dc], gbs.at[0], gbr.at[0], at(q, core))

    pieces = []
    for h in range(HALVES):
        if h == 1:
            halves.append(image_part(h, c))
        landed(part.at[h], fr.at[h])
        halves[h] = halves[h] + image_part(h, 1 - c)
        pieces += split2(halves[h])
        gram = mm(jnp.concatenate(pieces[-2:], 0), jnp.concatenate(pieces, 0), NT)
        gram = gram[:HALF] + gram[HALF:]
        for g in range(h + 1):
            block = gram[:, g * K:g * K + HALF] + gram[:, g * K + HALF:(g + 1) * K]
            gram_part[h + g] = block.reshape(PLANE, 8, 128)
        if h == 0:
            for s in range(1, PLANE):
                gram_a(s).start()

            @pl.when(jnp.logical_not(keeps_a))
            def _():
                gram_a(0).start()
        else:
            for s, dc in pairs:
                gram_b(s, dc).start()

    def gram_z_copy(store, send, recv, step):
        return remote(store.at[z], store.at[z], send.at[0], recv.at[0], device(x, mod(z + step, NZ), y, c))

    @pl.when(keeps_a)
    def _():
        total = gram_part[0, p]
        landed(gram_in_a.at[pl.ds(1, 31)], gar.at[0])
        for slot in range(1, 32):
            total = total + gram_in_a[slot]
        gram_z_a[z] = total
        for step in Z_STEPS:
            gram_z_copy(gram_z_a, has, har, step).start()

    total = gram_part[1 + c, p]
    landed(gram_in_b.at[pl.ds(1, 31)], gbr.at[0])
    for slot in range(1, 32):
        total = total + gram_in_b[slot]
    gram_z_b[z] = total
    for step in Z_STEPS:
        gram_z_copy(gram_z_b, hbs, hbr, step).start()

    image[...] = jnp.concatenate(halves, 0).T
    image_copy = pltpu.make_async_copy(image, image_hbm, out_sem.at[0])
    image_copy.start()
    for h in range(HALVES):
        core_copy(h).wait_send()
        landed(plane_in.at[h], xs.at[h])
        landed(plane_in.at[h], bs.at[h])
        landed(part.at[h], fs.at[h])
        for t in range(OWN_TILES):
            @pl.when(keeper(h, t) != z)
            def _(h=h, t=t):
                z_copy(h, t).wait_send()

        @pl.when(keeps(h))
        def _():
            landed(z_in.at[pl.ds(1, NZ - 1)], ags.at[0])
    for s in range(1, PLANE):
        gram_a(s).wait_send()

    @pl.when(jnp.logical_not(keeps_a))
    def _():
        gram_a(0).wait_send()

    landed(gram_in_b.at[pl.ds(1, 31)], gbs.at[0])

    def z_sum(store, recv):
        landed(store.at[pl.ds(0, NZ - 1)], recv.at[0])
        total = store[0]
        for i in range(1, NZ):
            total = total + store[i]
        return total

    def gram_out_a(s, dc):
        block = gram_a_all.at[p]
        return remote(block, block, kas.at[0], kar.at[0], at(offset(x, y, *around[s]), mod(c + dc, NC)))

    def gram_out_b(s, dc):
        other = at(offset(x, y, *around[s]), mod(c + dc, NC))
        return remote(gram_b_own, gram_hbm.at[c, p], kbs.at[0], kbr.at[0], other)

    @pl.when(keeps_a)
    def _():
        gram_a_all[p] = z_sum(gram_z_a, har)
        for s, dc in pairs:
            gram_out_a(s, dc).start()

    gram_b_own[...] = z_sum(gram_z_b, hbr)
    for s, dc in pairs:
        gram_out_b(s, dc).start()
    own_copy = pltpu.make_async_copy(gram_b_own, gram_hbm.at[c, p], out_sem.at[1])
    own_copy.start()

    @pl.when(keeps_a)
    def _():
        landed(gram_a_all.at[pl.ds(0, PLANE - 1)], kar.at[0])

    @pl.when(jnp.logical_not(keeps_a))
    def _():
        landed(gram_a_all, kar.at[0])

    first[...] = first_inverse(gram_a_all[...].reshape(HALF, HALF))
    first_copy = pltpu.make_async_copy(first, first_hbm, out_sem.at[2])
    first_copy.start()

    @pl.when(keeps_a)
    def _():
        landed(gram_z_a.at[pl.ds(0, NZ - 1)], has.at[0])
        landed(gram_in_a.at[pl.ds(1, 31)], kas.at[0])

    landed(gram_z_b.at[pl.ds(0, NZ - 1)], hbs.at[0])
    landed(gram_in_b.at[pl.ds(1, 31)], kbs.at[0])
    image_copy.wait()
    own_copy.wait()
    first_copy.wait()

    landed(gram_in_b.at[pl.ds(1, 31)], kbr.at[0])


def sums(embeddings, start_basis):
    rows = embeddings.shape[0]
    dma = lambda *n: pltpu.SemaphoreType.DMA(n)
    vmem = pltpu.VMEM
    return pl.pallas_call(
        gather_kernel,
        out_shape=(
            jax.ShapeDtypeStruct((rows, K), F32),
            jax.ShapeDtypeStruct((NC, PLANE, 8, 128), F32),
            jax.ShapeDtypeStruct((HALF, HALF), F32),
        ),
        in_specs=[pl.BlockSpec(memory_space=pl.ANY)] * 2,
        out_specs=(pl.BlockSpec(memory_space=pl.ANY),) * 3,
        scratch_shapes=[
            vmem((PARTS, rows, WIDE), F32),
            vmem((PARTS, rows, WIDE), BF16),
            vmem((PARTS, rows, WIDE), BF16),
            vmem((rows, K), F32),
            vmem((HALVES, PLANE, 8, OWN), F32),
            vmem((HALVES, PLANE, 8, OWN), F32),
            vmem((HALVES, PLANE, 8, OWN), F32),
            vmem((HALVES, PLANE - 1, 8, OWN), F32),
            vmem((HALVES, OWN_TILES, 8, 128), F32),
            vmem((NZ, 8, 128), F32),
            vmem((HALVES, PLANE, 8, D), F32),
            vmem((rows, K), F32),
            vmem((3, PLANE, 8, 128), F32),
            vmem((32, 8, 128), F32),
            vmem((32, 8, 128), F32),
            vmem((NZ, 8, 128), F32),
            vmem((NZ, 8, 128), F32),
            vmem((PLANE, 8, 128), F32),
            vmem((8, 128), F32),
            vmem((HALF, HALF), F32),
            dma(PARTS + 1),
            dma(HALVES), dma(HALVES),
            dma(HALVES), dma(HALVES),
            dma(HALVES, OWN_TILES), dma(1),
            dma(1), dma(HALVES, OWN_TILES),
            dma(HALVES), dma(HALVES, PLANE),
            dma(HALVES), dma(HALVES),
            dma(PLANE), dma(1),
            dma(1), dma(1),
            dma(1), dma(1),
            dma(1), dma(1),
            dma(1), dma(1),
            dma(1), dma(1),
            dma(3),
            pltpu.SemaphoreType.REGULAR,
        ],
        compiler_params=pltpu.CompilerParams(
            collective_id=0, has_side_effects=True, vmem_limit_bytes=VMEM_BYTES
        ),
        name="sums",
    )(embeddings, start_basis)


LEFT = (0, 0, 1, 0, 2, 1)
RIGHT = (0, 1, 0, 2, 0, 1)


def stacked(pieces, order):
    return jnp.concatenate([pieces[i] for i in order], 0)


def spread(block, size):
    return [jnp.broadcast_to(block[:, j:j + 1], (size, 128)) for j in range(size)]


def eliminate(panels):
    size = BLOCK
    rows = lax.broadcasted_iota(jnp.int32, (size, 128), 0)
    done = []
    strips = [panel[:size] for panel in panels]
    rest = [panel[size:] for panel in panels]
    for off in range(0, HALF, size):
        last = off + size == HALF
        cols = spread(strips[0][:, off:off + size], size)
        if not last:
            ahead = spread(strips[0][:, off + size:off + 2 * size].T, size)
            change = [0.0] * len(strips)
        scale = jnp.zeros((size, 128), F32)
        for j in range(0, size, 2):
            cj, cn = cols[j], cols[j + 1]
            a, b, d = cj[j:j + 1], cj[j + 1:j + 2], cn[j + 1:j + 2]
            q = 1.0 / (a * d - b * b)
            aq, bq, dq = a * q, b * q, d * q
            u = cj * dq - cn * bq
            v = cn * aq - cj * bq
            for k in range(j + 2, size):
                lo = (k // 8) * 8
                new = cols[k][lo:] - (u[lo:] * cj[k:k + 1] + v[lo:] * cn[k:k + 1])
                cols[k] = jnp.concatenate([cols[k][:lo], new], 0) if lo else new
            if not last:
                aj, an = ahead[j], ahead[j + 1]
                au = aj * dq - an * bq
                av = an * aq - aj * bq
                for k in range(j + 2, size):
                    ahead[k] = ahead[k] - (au * cj[k:k + 1] + av * cn[k:k + 1])
                change = [t + (au * s[j:j + 1] + av * s[j + 1:j + 2]) for t, s in zip(change, strips)]
            below = rows > j + 1
            ba = b * (1.0 / a)
            um = jnp.where(below, u, jnp.where(rows == j + 1, ba, 0.0))
            vm = jnp.where(below, v, 0.0)
            strips = [s - (um * s[j:j + 1] + vm * s[j + 1:j + 2]) for s in strips]
            ra = lax.rsqrt(a)
            rd = lax.rsqrt(d - ba * b)
            scale = jnp.where(rows == j, ra, jnp.where(rows == j + 1, rd, scale))
        strips = [s * scale for s in strips]
        done.append(strips[1:])
        if last:
            break
        following = [r[:size] - t for r, t in zip(rest, change)]
        behind = off + 2 * size
        if behind < HALF:
            pieces = [split3(s) for s in strips]
            left = stacked(pieces[0], LEFT)
            right = jnp.concatenate([stacked(piece, RIGHT) for piece in pieces], 1)
            product = mm(left, right, TN)[behind:]
            rest = [r[size:] - product[:, 128 * i:128 * (i + 1)] for i, r in enumerate(rest)]
        strips = following
    return [jnp.concatenate([strips[i] for strips in done], 0) for i in range(len(panels) - 1)]


def mm6(a, b, dims):
    ((left,), (right,)), _ = dims
    pa, pb = split3(a), split3(b)
    return mm(jnp.concatenate([pa[i] for i in LEFT], left), jnp.concatenate([pb[i] for i in RIGHT], right), dims)


def diagonal():
    return lax.broadcasted_iota(jnp.int32, (HALF, HALF), 0) == lax.broadcasted_iota(jnp.int32, (HALF, HALF), 1)


def diagonal_scales(value):
    entries = jnp.where(diagonal(), value, 0.0)
    return (
        lax.rsqrt(jnp.sum(entries, axis=1, keepdims=True)),
        lax.rsqrt(jnp.sum(entries, axis=0, keepdims=True)),
    )


def first_inverse(aa):
    col, row = diagonal_scales(aa)
    (inverse,) = eliminate([aa * col * row, jnp.where(diagonal(), 1.0, 0.0)])
    return inverse * row


def basis_kernel(scale, gram_hbm, first_hbm, image_hbm, out_hbm, gram, first_in, image, out, sems):
    loads = [
        pltpu.make_async_copy(src, dst, sems.at[i])
        for i, (src, dst) in enumerate([(gram_hbm, gram), (first_hbm, first_in), (image_hbm, image)])
    ]
    for copy in loads:
        copy.start()
    loads[0].wait()
    ba, bb = gram[0].reshape(HALF, HALF), gram[1].reshape(HALF, HALF)
    col, row = diagonal_scales(bb)
    loads[1].wait()
    first = first_in[...]
    cross = mm6(ba * col, first, NT)
    rest = bb * col * row - mm6(cross, cross, NT)
    lower = mm6(cross, first, NN)
    loads[2].wait()
    rows = image.shape[0]
    outs = []

    def product(value, factor):
        hi, lo = split2(value)
        high, low = split2(factor)
        both = mm(hi, jnp.concatenate([high, low], 0), NT)
        return both[:, :HALF] + (both[:, HALF:] + mm(lo, high, NT))

    def leave(r, n, cols):
        outs.append(pltpu.make_async_copy(out.at[pl.ds(r, n), cols], out_hbm.at[pl.ds(r, n), cols], sems.at[3 + len(outs)]))
        outs[-1].start()

    out[:, :HALF] = product(image[:, :HALF], first * scale)
    leave(0, rows, pl.ds(0, HALF))
    below, second = eliminate([rest, -lower, jnp.where(diagonal(), 1.0, 0.0)])
    factor = jnp.concatenate([below, second * row], 1) * scale
    step = rows // 2
    for r in range(0, rows, step):
        out[r:r + step, HALF:] = product(image[r:r + step, :], factor)
        leave(r, step, pl.ds(HALF, HALF))
    for copy in outs:
        copy.wait()


def basis_of(gram, first, image, scale):
    rows = image.shape[0]
    return pl.pallas_call(
        functools.partial(basis_kernel, scale),
        out_shape=jax.ShapeDtypeStruct((rows, K), F32),
        in_specs=[pl.BlockSpec(memory_space=pl.ANY)] * 3,
        out_specs=pl.BlockSpec(memory_space=pl.ANY),
        scratch_shapes=[
            pltpu.VMEM((NC, PLANE, 8, 128), F32),
            pltpu.VMEM((HALF, HALF), F32),
            pltpu.VMEM((rows, K), F32),
            pltpu.VMEM((rows, K), F32),
            pltpu.SemaphoreType.DMA((6,)),
        ],
        compiler_params=pltpu.CompilerParams(vmem_limit_bytes=VMEM_BYTES),
        name="basis",
    )(gram, first, image)


def local(embeddings, start_basis):
    total_rows = embeddings.shape[0] * lax.axis_size("dp")
    image, gram, first = sums(embeddings, start_basis)
    return basis_of(gram, first, image, float(total_rows) ** 0.5)


def solution(mesh):
    in_specs = (P("dp", None), P("dp", None))
    out_specs = P("dp", None)
    return jax.shard_map(local, mesh=mesh, in_specs=in_specs, out_specs=out_specs, check_vma=False)
```

```python
import functools

import jax
import jax.numpy as jnp
from jax import lax
from jax.experimental import pallas as pl
from jax.experimental.pallas import tpu as pltpu
from jax.sharding import PartitionSpec as P

F32, BF16 = jnp.float32, jnp.bfloat16
NX, NZ, NY, NC = 4, 16, 4, 2
PLANE = NX * NY
D, K = 1024, 256
PARTS = 4
WIDE = D // PARTS
HALVES = 2
HALF = K // HALVES
OWN = D // NC
OWN_TILES = OWN // 128
BLOCK = 16
VMEM_BYTES = 60 << 20

PLANE_STEPS = sorted(
    [(dx, dy) for dx in range(NX) for dy in range(NY) if (dx, dy) != (0, 0)],
    key=lambda s: -(min(s[0], NX - s[0]) + min(s[1], NY - s[1])),
)
PLANE_CORE_STEPS = [(dx, dy, dc) for dx, dy in PLANE_STEPS for dc in range(NC)] + [(0, 0, 1)]
Z_STEPS = sorted(range(1, NZ), key=lambda d: -min(d, NZ - d))

NT = (((1,), (1,)), ((), ()))
NN = (((1,), (0,)), ((), ()))
TN = (((0,), (0,)), ((), ()))


def mm(a, b, dims):
    return lax.dot_general(a, b, dims, preferred_element_type=F32)


def split2(value):
    high = value.astype(BF16)
    return high, (value - high.astype(F32)).astype(BF16)


def split3(value):
    high = value.astype(BF16)
    rest = value - high.astype(F32)
    middle = rest.astype(BF16)
    return high, middle, (rest - middle.astype(F32)).astype(BF16)


def device(x, z, y, c):
    return ((x * NZ + z) * NY + y) * NC + c


def remote(src, dst, send, recv, target):
    return pltpu.make_async_remote_copy(
        src_ref=src,
        dst_ref=dst,
        send_sem=send,
        recv_sem=recv,
        device_id={"dp": target},
        device_id_type=pl.DeviceIdType.MESH,
    )


def mod(value, n):
    return lax.rem(value, n)


def offset(x, y, dx, dy):
    return mod(x + dx % NX, NX) * NY + mod(y + dy % NY, NY)


def landed(ref, sem):
    pltpu.make_async_copy(ref, ref, sem).wait()


def gather_kernel(
    emb_hbm, start_hbm, image_hbm, gram_hbm, first_hbm,
    emb, emb_hi, emb_lo, start, give, core_in, part, plane_in, tiles, z_in, sketch,
    image, gram_part, gram_in_a, gram_in_b, gram_z_a, gram_z_b, gram_a_all, gram_b_own, first,
    load_sem, core_s, core_r, xs, xr, zs, zr, ags, agr, bs, br, fs, fr,
    gas, gar, gbs, gbr, has, har, hbs, hbr, kas, kar, kbs, kbr, out_sem, relay,
):
    me = lax.axis_index("dp")
    x, z, y, c = lax.div(me, NZ * NY * NC), mod(lax.div(me, NY * NC), NZ), mod(lax.div(me, NC), NY), mod(me, NC)
    p = x * NY + y
    sibling = device(x, z, y, 1 - c)
    around = [(0, 0)] + PLANE_STEPS

    def at(q, core):
        return device(lax.div(q, NY), z, mod(q, NY), core)

    places = [NC * (1 - c), NC * (1 - c) + 1, NC * c, NC * c + 1]

    def wide(i):
        return pl.ds(pl.multiple_of(places[i] * WIDE, WIDE), WIDE)

    loads = [pltpu.make_async_copy(start_hbm, start, load_sem.at[PARTS])]
    loads += [pltpu.make_async_copy(emb_hbm.at[:, wide(i)], emb.at[i], load_sem.at[i]) for i in range(PARTS)]
    for copy in loads:
        copy.start()

    barrier = pltpu.get_barrier_semaphore()
    greeted = [device(x, mod(z + step, NZ), y, c) for step in Z_STEPS if min(step, NZ - step) <= NZ // 4]
    greeted += [at(offset(x, y, dx, dy), mod(c + dc, NC)) for dx, dy, dc in PLANE_CORE_STEPS]
    for other in greeted:
        pl.semaphore_signal(barrier, inc=1, device_id={"dp": other}, device_id_type=pl.DeviceIdType.MESH)

    loads[0].wait()
    start_hi, start_lo = split2(start[...].T)

    def core_copy(h):
        return remote(give.at[h], core_in.at[h], core_s.at[h], core_r.at[h], sibling)

    for i in range(PARTS):
        if i == NC:
            pl.semaphore_wait(barrier, len(greeted))
            for h in range(HALVES):
                core_copy(h).start()
        loads[1 + i].wait()
        hi, lo = split2(emb[i])
        emb_hi[i] = hi
        emb_lo[i] = lo
        total = mm(start_hi, hi, NN) + (mm(start_hi, lo, NN) + mm(start_lo, hi, NN))
        store, j = (give, i) if i < NC else (part, i - NC)
        store[:, :, :, j * WIDE:(j + 1) * WIDE] = total.reshape(HALVES, PLANE, 8, WIDE)

    for step in (NZ // 4, NZ - NZ // 4):
        pl.semaphore_signal(relay, inc=1, device_id={"dp": device(x, mod(z + step, NZ), y, c)}, device_id_type=pl.DeviceIdType.MESH)

    def plane_copy(h, o):
        q = offset(x, y, *PLANE_STEPS[o])
        return remote(part.at[h, q], plane_in.at[h, o], xs.at[h], xr.at[h], at(q, c))

    for h in range(HALVES):
        core_copy(h).wait_recv()
        part[h] = part[h] + core_in[h]
        for o in range(PLANE - 1):
            plane_copy(h, o).start()

    pl.semaphore_wait(relay, 2)

    def keeper(h, t):
        return 4 * t + NC * h + c

    def z_copy(h, t):
        step = mod(keeper(h, t) - z + NZ, NZ)
        return remote(tiles.at[h, t], z_in.at[step], zs.at[h, t], zr.at[0], device(x, keeper(h, t), y, c))

    for h in range(HALVES):
        landed(plane_in.at[h], xr.at[h])
        total = part[h, p]
        for o in range(PLANE - 1):
            total = total + plane_in[h, o]
        for t in range(OWN_TILES):
            tiles[h, t] = total[:, t * 128:(t + 1) * 128]
        for t in range(OWN_TILES):
            @pl.when(keeper(h, t) != z)
            def _(h=h, t=t):
                z_copy(h, t).start()

    def lanes(start, size):
        return pl.ds(pl.multiple_of(start, 128), size)

    def tile_of(h, t):
        return sketch.at[h, p, :, lanes(c * OWN + t * 128, 128)]

    mine = lax.div(z, 4)

    def z_out(h, step):
        return remote(tile_of(h, mine), tile_of(h, mine), ags.at[0], agr.at[h, mine], device(x, mod(z + step, NZ), y, c))

    def keeps(h):
        return mod(z, 4) == NC * h + c

    for h in range(HALVES):
        @pl.when(keeps(h))
        def _(h=h):
            landed(z_in.at[pl.ds(1, NZ - 1)], zr.at[0])
            total = tiles[h, mine]
            for step in range(1, NZ):
                total = total + z_in[step]
            sketch[h, p, :, lanes(c * OWN + mine * 128, 128)] = total
            for step in Z_STEPS:
                z_out(h, step).start()

    def block_of(h, q, core):
        return sketch.at[h, q, :, lanes(core * OWN, OWN)]

    def plane_out(h, o):
        q = offset(x, y, *PLANE_STEPS[o])
        return remote(block_of(h, p, c), block_of(h, p, c), bs.at[h], br.at[h, o], at(q, c))

    def source(o):
        if o == PLANE - 1:
            return p
        dx, dy = PLANE_STEPS[o]
        return offset(x, y, -dx, -dy)

    def forward(h, o):
        return remote(block_of(h, source(o), c), block_of(h, source(o), c), fs.at[h], fr.at[h], sibling)

    for h in range(HALVES):
        for t in range(OWN_TILES):
            @pl.when(keeper(h, t) != z)
            def _(h=h, t=t):
                landed(tile_of(h, t), agr.at[h, t])
        for o in range(PLANE - 1):
            plane_out(h, o).start()
        forward(h, PLANE - 1).start()

    def image_part(h, core):
        total = None
        for j in range(NC):
            i = (NC if core is c else 0) + j
            block = sketch[h, :, :, lanes(core * OWN + j * WIDE, WIDE)]
            hi, lo = split2(block.reshape(HALF, WIDE))
            both = mm(jnp.concatenate([hi, lo], 0), emb_hi[i], NT)
            term = both[:HALF] + (both[HALF:] + mm(hi, emb_lo[i], NT))
            total = term if total is None else total + term
        return total

    halves = []
    def pass_on(h):
        for o in reversed(range(PLANE - 1)):
            block = block_of(h, source(o), c)
            landed(block, br.at[h, o])
            forward(h, o).start()

    pass_on(0)
    halves.append(image_part(0, c))

    keeps_a = mod(y, NC) == c

    pairs = [(s, dc) for s in range(PLANE) for dc in range(NC) if (s, dc) != (0, 0)]

    def gram_a(s):
        q = offset(x, y, *around[s])
        slot = NC * s + mod(q + c, NC)
        return remote(gram_part.at[0, q], gram_in_a.at[slot], gas.at[s], gar.at[0], at(q, mod(q, NC)))

    def gram_b(s, dc):
        q, core = offset(x, y, *around[s]), mod(c + dc, NC)
        return remote(gram_part.at[1 + core, q], gram_in_b.at[NC * s + dc], gbs.at[0], gbr.at[0], at(q, core))

    pieces = []
    for h in range(HALVES):
        if h == 1:
            pass_on(h)
            halves.append(image_part(h, c))
        landed(part.at[h], fr.at[h])
        halves[h] = halves[h] + image_part(h, 1 - c)
        pieces += split2(halves[h])
        gram = mm(jnp.concatenate(pieces[-2:], 0), jnp.concatenate(pieces, 0), NT)
        gram = gram[:HALF] + gram[HALF:]
        for g in range(h + 1):
            block = gram[:, g * K:g * K + HALF] + gram[:, g * K + HALF:(g + 1) * K]
            gram_part[h + g] = block.reshape(PLANE, 8, 128)
        if h == 0:
            for s in range(1, PLANE):
                gram_a(s).start()

            @pl.when(jnp.logical_not(keeps_a))
            def _():
                gram_a(0).start()
        else:
            for s, dc in pairs:
                gram_b(s, dc).start()

    def gram_z_copy(store, send, recv, step):
        return remote(store.at[z], store.at[z], send.at[0], recv.at[0], device(x, mod(z + step, NZ), y, c))

    @pl.when(keeps_a)
    def _():
        total = gram_part[0, p]
        landed(gram_in_a.at[pl.ds(1, 31)], gar.at[0])
        for slot in range(1, 32):
            total = total + gram_in_a[slot]
        gram_z_a[z] = total
        for step in Z_STEPS:
            gram_z_copy(gram_z_a, has, har, step).start()

    total = gram_part[1 + c, p]
    landed(gram_in_b.at[pl.ds(1, 31)], gbr.at[0])
    for slot in range(1, 32):
        total = total + gram_in_b[slot]
    gram_z_b[z] = total
    for step in Z_STEPS:
        gram_z_copy(gram_z_b, hbs, hbr, step).start()

    image[...] = jnp.concatenate(halves, 0).T
    image_copy = pltpu.make_async_copy(image, image_hbm, out_sem.at[0])
    image_copy.start()
    for h in range(HALVES):
        core_copy(h).wait_send()
        landed(plane_in.at[h], xs.at[h])
        landed(plane_in.at[h], bs.at[h])
        landed(part.at[h], fs.at[h])
        for t in range(OWN_TILES):
            @pl.when(keeper(h, t) != z)
            def _(h=h, t=t):
                z_copy(h, t).wait_send()

        @pl.when(keeps(h))
        def _():
            landed(z_in.at[pl.ds(1, NZ - 1)], ags.at[0])
    for s in range(1, PLANE):
        gram_a(s).wait_send()

    @pl.when(jnp.logical_not(keeps_a))
    def _():
        gram_a(0).wait_send()

    landed(gram_in_b.at[pl.ds(1, 31)], gbs.at[0])

    def z_sum(store, recv):
        landed(store.at[pl.ds(0, NZ - 1)], recv.at[0])
        total = store[0]
        for i in range(1, NZ):
            total = total + store[i]
        return total

    def gram_out_a(s, dc):
        block = gram_a_all.at[p]
        return remote(block, block, kas.at[0], kar.at[0], at(offset(x, y, *around[s]), mod(c + dc, NC)))

    def gram_out_b(s, dc):
        other = at(offset(x, y, *around[s]), mod(c + dc, NC))
        return remote(gram_b_own, gram_hbm.at[c, p], kbs.at[0], kbr.at[0], other)

    @pl.when(keeps_a)
    def _():
        gram_a_all[p] = z_sum(gram_z_a, har)
        for s, dc in pairs:
            gram_out_a(s, dc).start()

    gram_b_own[...] = z_sum(gram_z_b, hbr)
    for s, dc in pairs:
        gram_out_b(s, dc).start()
    own_copy = pltpu.make_async_copy(gram_b_own, gram_hbm.at[c, p], out_sem.at[1])
    own_copy.start()

    @pl.when(keeps_a)
    def _():
        landed(gram_a_all.at[pl.ds(0, PLANE - 1)], kar.at[0])

    @pl.when(jnp.logical_not(keeps_a))
    def _():
        landed(gram_a_all, kar.at[0])

    first[...] = first_inverse(gram_a_all[...].reshape(HALF, HALF))
    first_copy = pltpu.make_async_copy(first, first_hbm, out_sem.at[2])
    first_copy.start()

    @pl.when(keeps_a)
    def _():
        landed(gram_z_a.at[pl.ds(0, NZ - 1)], has.at[0])
        landed(gram_in_a.at[pl.ds(1, 31)], kas.at[0])

    landed(gram_z_b.at[pl.ds(0, NZ - 1)], hbs.at[0])
    landed(gram_in_b.at[pl.ds(1, 31)], kbs.at[0])
    image_copy.wait()
    own_copy.wait()
    first_copy.wait()

    landed(gram_in_b.at[pl.ds(1, 31)], kbr.at[0])


def sums(embeddings, start_basis):
    rows = embeddings.shape[0]
    dma = lambda *n: pltpu.SemaphoreType.DMA(n)
    vmem = pltpu.VMEM
    return pl.pallas_call(
        gather_kernel,
        out_shape=(
            jax.ShapeDtypeStruct((rows, K), F32),
            jax.ShapeDtypeStruct((NC, PLANE, 8, 128), F32),
            jax.ShapeDtypeStruct((HALF, HALF), F32),
        ),
        in_specs=[pl.BlockSpec(memory_space=pl.ANY)] * 2,
        out_specs=(pl.BlockSpec(memory_space=pl.ANY),) * 3,
        scratch_shapes=[
            vmem((PARTS, rows, WIDE), F32),
            vmem((PARTS, rows, WIDE), BF16),
            vmem((PARTS, rows, WIDE), BF16),
            vmem((rows, K), F32),
            vmem((HALVES, PLANE, 8, OWN), F32),
            vmem((HALVES, PLANE, 8, OWN), F32),
            vmem((HALVES, PLANE, 8, OWN), F32),
            vmem((HALVES, PLANE - 1, 8, OWN), F32),
            vmem((HALVES, OWN_TILES, 8, 128), F32),
            vmem((NZ, 8, 128), F32),
            vmem((HALVES, PLANE, 8, D), F32),
            vmem((rows, K), F32),
            vmem((3, PLANE, 8, 128), F32),
            vmem((32, 8, 128), F32),
            vmem((32, 8, 128), F32),
            vmem((NZ, 8, 128), F32),
            vmem((NZ, 8, 128), F32),
            vmem((PLANE, 8, 128), F32),
            vmem((8, 128), F32),
            vmem((HALF, HALF), F32),
            dma(PARTS + 1),
            dma(HALVES), dma(HALVES),
            dma(HALVES), dma(HALVES),
            dma(HALVES, OWN_TILES), dma(1),
            dma(1), dma(HALVES, OWN_TILES),
            dma(HALVES), dma(HALVES, PLANE),
            dma(HALVES), dma(HALVES),
            dma(PLANE), dma(1),
            dma(1), dma(1),
            dma(1), dma(1),
            dma(1), dma(1),
            dma(1), dma(1),
            dma(1), dma(1),
            dma(3),
            pltpu.SemaphoreType.REGULAR,
        ],
        compiler_params=pltpu.CompilerParams(
            collective_id=0, has_side_effects=True, vmem_limit_bytes=VMEM_BYTES
        ),
        name="sums",
    )(embeddings, start_basis)


LEFT = (0, 0, 1, 0, 2, 1)
RIGHT = (0, 1, 0, 2, 0, 1)


def stacked(pieces, order):
    return jnp.concatenate([pieces[i] for i in order], 0)


def spread(block, size):
    return [jnp.broadcast_to(block[:, j:j + 1], (size, 128)) for j in range(size)]


def eliminate(panels):
    size = BLOCK
    rows = lax.broadcasted_iota(jnp.int32, (size, 128), 0)
    done = []
    strips = [panel[:size] for panel in panels]
    rest = [panel[size:] for panel in panels]
    for off in range(0, HALF, size):
        last = off + size == HALF
        cols = spread(strips[0][:, off:off + size], size)
        if not last:
            ahead = spread(strips[0][:, off + size:off + 2 * size].T, size)
            change = [0.0] * len(strips)
        scale = jnp.zeros((size, 128), F32)
        for j in range(0, size, 2):
            cj, cn = cols[j], cols[j + 1]
            a, b, d = cj[j:j + 1], cj[j + 1:j + 2], cn[j + 1:j + 2]
            q = 1.0 / (a * d - b * b)
            aq, bq, dq = a * q, b * q, d * q
            u = cj * dq - cn * bq
            v = cn * aq - cj * bq
            for k in range(j + 2, size):
                lo = (k // 8) * 8
                new = cols[k][lo:] - (u[lo:] * cj[k:k + 1] + v[lo:] * cn[k:k + 1])
                cols[k] = jnp.concatenate([cols[k][:lo], new], 0) if lo else new
            if not last:
                aj, an = ahead[j], ahead[j + 1]
                au = aj * dq - an * bq
                av = an * aq - aj * bq
                for k in range(j + 2, size):
                    ahead[k] = ahead[k] - (au * cj[k:k + 1] + av * cn[k:k + 1])
                change = [t + (au * s[j:j + 1] + av * s[j + 1:j + 2]) for t, s in zip(change, strips)]
            below = rows > j + 1
            ba = b * (1.0 / a)
            um = jnp.where(below, u, jnp.where(rows == j + 1, ba, 0.0))
            vm = jnp.where(below, v, 0.0)
            strips = [s - (um * s[j:j + 1] + vm * s[j + 1:j + 2]) for s in strips]
            ra = lax.rsqrt(a)
            rd = lax.rsqrt(d - ba * b)
            scale = jnp.where(rows == j, ra, jnp.where(rows == j + 1, rd, scale))
        strips = [s * scale for s in strips]
        done.append(strips[1:])
        if last:
            break
        following = [r[:size] - t for r, t in zip(rest, change)]
        behind = off + 2 * size
        if behind < HALF:
            pieces = [split3(s) for s in strips]
            left = stacked(pieces[0], LEFT)
            right = jnp.concatenate([stacked(piece, RIGHT) for piece in pieces], 1)
            product = mm(left, right, TN)[behind:]
            rest = [r[size:] - product[:, 128 * i:128 * (i + 1)] for i, r in enumerate(rest)]
        strips = following
    return [jnp.concatenate([strips[i] for strips in done], 0) for i in range(len(panels) - 1)]


def mm6(a, b, dims):
    ((left,), (right,)), _ = dims
    pa, pb = split3(a), split3(b)
    return mm(jnp.concatenate([pa[i] for i in LEFT], left), jnp.concatenate([pb[i] for i in RIGHT], right), dims)


def diagonal():
    return lax.broadcasted_iota(jnp.int32, (HALF, HALF), 0) == lax.broadcasted_iota(jnp.int32, (HALF, HALF), 1)


def diagonal_scales(value):
    entries = jnp.where(diagonal(), value, 0.0)
    return (
        lax.rsqrt(jnp.sum(entries, axis=1, keepdims=True)),
        lax.rsqrt(jnp.sum(entries, axis=0, keepdims=True)),
    )


def first_inverse(aa):
    col, row = diagonal_scales(aa)
    (inverse,) = eliminate([aa * col * row, jnp.where(diagonal(), 1.0, 0.0)])
    return inverse * row


def basis_kernel(scale, gram_hbm, first_hbm, image_hbm, out_hbm, gram, first_in, image, out, sems):
    loads = [
        pltpu.make_async_copy(src, dst, sems.at[i])
        for i, (src, dst) in enumerate([(gram_hbm, gram), (first_hbm, first_in), (image_hbm, image)])
    ]
    for copy in loads:
        copy.start()
    loads[0].wait()
    ba, bb = gram[0].reshape(HALF, HALF), gram[1].reshape(HALF, HALF)
    col, row = diagonal_scales(bb)
    loads[1].wait()
    first = first_in[...]
    cross = mm6(ba * col, first, NT)
    rest = bb * col * row - mm6(cross, cross, NT)
    lower = mm6(cross, first, NN)
    loads[2].wait()
    rows = image.shape[0]
    outs = []

    def product(value, factor):
        hi, lo = split2(value)
        high, low = split2(factor)
        both = mm(hi, jnp.concatenate([high, low], 0), NT)
        return both[:, :HALF] + (both[:, HALF:] + mm(lo, high, NT))

    def leave(r, n, cols):
        outs.append(pltpu.make_async_copy(out.at[pl.ds(r, n), cols], out_hbm.at[pl.ds(r, n), cols], sems.at[3 + len(outs)]))
        outs[-1].start()

    out[:, :HALF] = product(image[:, :HALF], first * scale)
    leave(0, rows, pl.ds(0, HALF))
    below, second = eliminate([rest, -lower, jnp.where(diagonal(), 1.0, 0.0)])
    factor = jnp.concatenate([below, second * row], 1) * scale
    step = rows // 2
    for r in range(0, rows, step):
        out[r:r + step, HALF:] = product(image[r:r + step, :], factor)
        leave(r, step, pl.ds(HALF, HALF))
    for copy in outs:
        copy.wait()


def basis_of(gram, first, image, scale):
    rows = image.shape[0]
    return pl.pallas_call(
        functools.partial(basis_kernel, scale),
        out_shape=jax.ShapeDtypeStruct((rows, K), F32),
        in_specs=[pl.BlockSpec(memory_space=pl.ANY)] * 3,
        out_specs=pl.BlockSpec(memory_space=pl.ANY),
        scratch_shapes=[
            pltpu.VMEM((NC, PLANE, 8, 128), F32),
            pltpu.VMEM((HALF, HALF), F32),
            pltpu.VMEM((rows, K), F32),
            pltpu.VMEM((rows, K), F32),
            pltpu.SemaphoreType.DMA((6,)),
        ],
        compiler_params=pltpu.CompilerParams(vmem_limit_bytes=VMEM_BYTES),
        name="basis",
    )(gram, first, image)


def local(embeddings, start_basis):
    total_rows = embeddings.shape[0] * lax.axis_size("dp")
    image, gram, first = sums(embeddings, start_basis)
    return basis_of(gram, first, image, float(total_rows) ** 0.5)


def solution(mesh):
    in_specs = (P("dp", None), P("dp", None))
    out_specs = P("dp", None)
    return jax.shard_map(local, mesh=mesh, in_specs=in_specs, out_specs=out_specs, check_vma=False)
```

```python
import functools

import jax
import jax.numpy as jnp
from jax import lax
from jax.experimental import pallas as pl
from jax.experimental.pallas import tpu as pltpu
from jax.sharding import PartitionSpec as P

F32, BF16 = jnp.float32, jnp.bfloat16
NX, NZ, NY, NC = 4, 16, 4, 2
PLANE = NX * NY
D, K = 1024, 256
PARTS = 4
WIDE = D // PARTS
HALVES = 2
HALF = K // HALVES
OWN = D // NC
OWN_TILES = OWN // 128
BLOCK = 16
VMEM_BYTES = 60 << 20

PLANE_STEPS = sorted(
    [(dx, dy) for dx in range(NX) for dy in range(NY) if (dx, dy) != (0, 0)],
    key=lambda s: -(min(s[0], NX - s[0]) + min(s[1], NY - s[1])),
)
PLANE_CORE_STEPS = [(dx, dy, dc) for dx, dy in PLANE_STEPS for dc in range(NC)] + [(0, 0, 1)]
Z_STEPS = sorted(range(1, NZ), key=lambda d: -min(d, NZ - d))

NT = (((1,), (1,)), ((), ()))
NN = (((1,), (0,)), ((), ()))
TN = (((0,), (0,)), ((), ()))


def mm(a, b, dims):
    return lax.dot_general(a, b, dims, preferred_element_type=F32)


def split2(value):
    high = value.astype(BF16)
    return high, (value - high.astype(F32)).astype(BF16)


def split3(value):
    high = value.astype(BF16)
    rest = value - high.astype(F32)
    middle = rest.astype(BF16)
    return high, middle, (rest - middle.astype(F32)).astype(BF16)


def device(x, z, y, c):
    return ((x * NZ + z) * NY + y) * NC + c


def remote(src, dst, send, recv, target):
    return pltpu.make_async_remote_copy(
        src_ref=src,
        dst_ref=dst,
        send_sem=send,
        recv_sem=recv,
        device_id={"dp": target},
        device_id_type=pl.DeviceIdType.MESH,
    )


def mod(value, n):
    return lax.rem(value, n)


def offset(x, y, dx, dy):
    return mod(x + dx % NX, NX) * NY + mod(y + dy % NY, NY)


def landed(ref, sem):
    pltpu.make_async_copy(ref, ref, sem).wait()


def gather_kernel(
    emb_hbm, start_hbm, image_hbm, gram_hbm, first_hbm,
    emb, emb_hi, emb_lo, start, give, core_in, part, plane_in, tiles, z_in, sketch,
    image, gram_part, gram_in_a, gram_in_b, gram_z_a, gram_z_b, gram_a_all, gram_b_own, first,
    load_sem, core_s, core_r, xs, xr, zs, zr, ags, agr, bs, br, fs, fr,
    gas, gar, gbs, gbr, has, har, hbs, hbr, kas, kar, kbs, kbr, out_sem, relay,
):
    me = lax.axis_index("dp")
    x, z, y, c = lax.div(me, NZ * NY * NC), mod(lax.div(me, NY * NC), NZ), mod(lax.div(me, NC), NY), mod(me, NC)
    p = x * NY + y
    sibling = device(x, z, y, 1 - c)
    around = [(0, 0)] + PLANE_STEPS

    def at(q, core):
        return device(lax.div(q, NY), z, mod(q, NY), core)

    places = [NC * (1 - c), NC * (1 - c) + 1, NC * c, NC * c + 1]

    def wide(i):
        return pl.ds(pl.multiple_of(places[i] * WIDE, WIDE), WIDE)

    loads = [pltpu.make_async_copy(start_hbm, start, load_sem.at[PARTS])]
    loads += [pltpu.make_async_copy(emb_hbm.at[:, wide(i)], emb.at[i], load_sem.at[i]) for i in range(PARTS)]
    for copy in loads:
        copy.start()

    barrier = pltpu.get_barrier_semaphore()
    greeted = [device(x, mod(z + step, NZ), y, c) for step in Z_STEPS if min(step, NZ - step) <= NZ // 4]
    greeted += [at(offset(x, y, dx, dy), mod(c + dc, NC)) for dx, dy, dc in PLANE_CORE_STEPS]
    for other in greeted:
        pl.semaphore_signal(barrier, inc=1, device_id={"dp": other}, device_id_type=pl.DeviceIdType.MESH)

    loads[0].wait()
    start_hi, start_lo = split2(start[...].T)

    def core_copy(h):
        return remote(give.at[h], core_in.at[h], core_s.at[h], core_r.at[h], sibling)

    for i in range(PARTS):
        if i == NC:
            pl.semaphore_wait(barrier, len(greeted))
            for h in range(HALVES):
                core_copy(h).start()
        loads[1 + i].wait()
        hi, lo = split2(emb[i])
        emb_hi[i] = hi
        emb_lo[i] = lo
        total = mm(start_hi, hi, NN) + (mm(start_hi, lo, NN) + mm(start_lo, hi, NN))
        store, j = (give, i) if i < NC else (part, i - NC)
        store[:, :, :, j * WIDE:(j + 1) * WIDE] = total.reshape(HALVES, PLANE, 8, WIDE)

    for step in (NZ // 4, NZ - NZ // 4):
        pl.semaphore_signal(relay, inc=1, device_id={"dp": device(x, mod(z + step, NZ), y, c)}, device_id_type=pl.DeviceIdType.MESH)

    def plane_copy(h, o):
        q = offset(x, y, *PLANE_STEPS[o])
        return remote(part.at[h, q], plane_in.at[h, o], xs.at[h], xr.at[h], at(q, c))

    for h in range(HALVES):
        core_copy(h).wait_recv()
        part[h] = part[h] + core_in[h]
        for o in range(PLANE - 1):
            plane_copy(h, o).start()

    pl.semaphore_wait(relay, 2)

    def keeper(h, t):
        return 4 * t + NC * h + c

    def z_copy(h, t):
        step = mod(keeper(h, t) - z + NZ, NZ)
        return remote(tiles.at[h, t], z_in.at[step], zs.at[h, t], zr.at[0], device(x, keeper(h, t), y, c))

    for h in range(HALVES):
        landed(plane_in.at[h], xr.at[h])
        total = part[h, p]
        for o in range(PLANE - 1):
            total = total + plane_in[h, o]
        for t in range(OWN_TILES):
            tiles[h, t] = total[:, t * 128:(t + 1) * 128]
        for t in range(OWN_TILES):
            @pl.when(keeper(h, t) != z)
            def _(h=h, t=t):
                z_copy(h, t).start()

    def lanes(start, size):
        return pl.ds(pl.multiple_of(start, 128), size)

    def tile_of(h, t):
        return sketch.at[h, p, :, lanes(c * OWN + t * 128, 128)]

    mine = lax.div(z, 4)

    def z_out(h, step):
        return remote(tile_of(h, mine), tile_of(h, mine), ags.at[0], agr.at[h, mine], device(x, mod(z + step, NZ), y, c))

    def keeps(h):
        return mod(z, 4) == NC * h + c

    for h in range(HALVES):
        @pl.when(keeps(h))
        def _(h=h):
            landed(z_in.at[pl.ds(1, NZ - 1)], zr.at[0])
            total = tiles[h, mine]
            for step in range(1, NZ):
                total = total + z_in[step]
            sketch[h, p, :, lanes(c * OWN + mine * 128, 128)] = total
            for step in Z_STEPS:
                z_out(h, step).start()

    def block_of(h, q, core):
        return sketch.at[h, q, :, lanes(core * OWN, OWN)]

    def plane_out(h, o):
        q = offset(x, y, *PLANE_STEPS[o])
        return remote(block_of(h, p, c), block_of(h, p, c), bs.at[h], br.at[h, o], at(q, c))

    def source(o):
        if o == PLANE - 1:
            return p
        dx, dy = PLANE_STEPS[o]
        return offset(x, y, -dx, -dy)

    def forward(h, o):
        return remote(block_of(h, source(o), c), block_of(h, source(o), c), fs.at[h], fr.at[h], sibling)

    for h in range(HALVES):
        for t in range(OWN_TILES):
            @pl.when(keeper(h, t) != z)
            def _(h=h, t=t):
                landed(tile_of(h, t), agr.at[h, t])
        for o in range(PLANE - 1):
            plane_out(h, o).start()
        forward(h, PLANE - 1).start()

    def image_part(h, core):
        total = None
        for j in range(NC):
            i = (NC if core is c else 0) + j
            block = sketch[h, :, :, lanes(core * OWN + j * WIDE, WIDE)]
            hi, lo = split2(block.reshape(HALF, WIDE))
            both = mm(jnp.concatenate([hi, lo], 0), emb_hi[i], NT)
            term = both[:HALF] + (both[HALF:] + mm(hi, emb_lo[i], NT))
            total = term if total is None else total + term
        return total

    halves = []
    def pass_on(h):
        for o in reversed(range(PLANE - 1)):
            block = block_of(h, source(o), c)
            landed(block, br.at[h, o])
            forward(h, o).start()

    pass_on(0)
    halves.append(image_part(0, c))

    keeps_a = mod(y, NC) == c

    pairs = [(s, dc) for s in range(1, PLANE) for dc in range(NC)] + [(0, 1)]

    def gram_a(s):
        q = offset(x, y, *around[s])
        slot = NC * s + mod(q + c, NC)
        return remote(gram_part.at[0, q], gram_in_a.at[slot], gas.at[s], gar.at[0], at(q, mod(q, NC)))

    def gram_b(s, dc):
        q, core = offset(x, y, *around[s]), mod(c + dc, NC)
        return remote(gram_part.at[1 + core, q], gram_in_b.at[NC * s + dc], gbs.at[0], gbr.at[0], at(q, core))

    pieces = []
    for h in range(HALVES):
        if h == 1:
            pass_on(h)
            halves.append(image_part(h, c))
        landed(part.at[h], fr.at[h])
        halves[h] = halves[h] + image_part(h, 1 - c)
        pieces += split2(halves[h])
        gram = mm(jnp.concatenate(pieces[-2:], 0), jnp.concatenate(pieces, 0), NT)
        gram = gram[:HALF] + gram[HALF:]
        for g in range(h + 1):
            block = gram[:, g * K:g * K + HALF] + gram[:, g * K + HALF:(g + 1) * K]
            gram_part[h + g] = block.reshape(PLANE, 8, 128)
        if h == 0:
            for s in range(1, PLANE):
                gram_a(s).start()

            @pl.when(jnp.logical_not(keeps_a))
            def _():
                gram_a(0).start()
        else:
            for s, dc in pairs:
                gram_b(s, dc).start()

    def gram_z_copy(store, send, recv, step):
        return remote(store.at[z], store.at[z], send.at[0], recv.at[0], device(x, mod(z + step, NZ), y, c))

    @pl.when(keeps_a)
    def _():
        total = gram_part[0, p]
        landed(gram_in_a.at[pl.ds(1, 31)], gar.at[0])
        for slot in range(1, 32):
            total = total + gram_in_a[slot]
        gram_z_a[z] = total
        for step in Z_STEPS:
            gram_z_copy(gram_z_a, has, har, step).start()

    total = gram_part[1 + c, p]
    landed(gram_in_b.at[pl.ds(1, 31)], gbr.at[0])
    for slot in range(1, 32):
        total = total + gram_in_b[slot]
    gram_z_b[z] = total
    for step in Z_STEPS:
        gram_z_copy(gram_z_b, hbs, hbr, step).start()

    image[...] = jnp.concatenate(halves, 0).T
    image_copy = pltpu.make_async_copy(image, image_hbm, out_sem.at[0])
    image_copy.start()
    for h in range(HALVES):
        core_copy(h).wait_send()
        landed(plane_in.at[h], xs.at[h])
        landed(plane_in.at[h], bs.at[h])
        landed(part.at[h], fs.at[h])
        for t in range(OWN_TILES):
            @pl.when(keeper(h, t) != z)
            def _(h=h, t=t):
                z_copy(h, t).wait_send()

        @pl.when(keeps(h))
        def _():
            landed(z_in.at[pl.ds(1, NZ - 1)], ags.at[0])
    for s in range(1, PLANE):
        gram_a(s).wait_send()

    @pl.when(jnp.logical_not(keeps_a))
    def _():
        gram_a(0).wait_send()

    landed(gram_in_b.at[pl.ds(1, 31)], gbs.at[0])

    def z_sum(store, recv):
        landed(store.at[pl.ds(0, NZ - 1)], recv.at[0])
        total = store[0]
        for i in range(1, NZ):
            total = total + store[i]
        return total

    def gram_out_a(s, dc):
        block = gram_a_all.at[p]
        return remote(block, block, kas.at[0], kar.at[0], at(offset(x, y, *around[s]), mod(c + dc, NC)))

    def gram_out_b(s, dc):
        other = at(offset(x, y, *around[s]), mod(c + dc, NC))
        return remote(gram_b_own, gram_hbm.at[c, p], kbs.at[0], kbr.at[0], other)

    @pl.when(keeps_a)
    def _():
        gram_a_all[p] = z_sum(gram_z_a, har)
        for s, dc in pairs:
            gram_out_a(s, dc).start()

    gram_b_own[...] = z_sum(gram_z_b, hbr)
    for s, dc in pairs:
        gram_out_b(s, dc).start()
    own_copy = pltpu.make_async_copy(gram_b_own, gram_hbm.at[c, p], out_sem.at[1])
    own_copy.start()

    @pl.when(keeps_a)
    def _():
        landed(gram_a_all.at[pl.ds(0, PLANE - 1)], kar.at[0])

    @pl.when(jnp.logical_not(keeps_a))
    def _():
        landed(gram_a_all, kar.at[0])

    first[...] = first_inverse(gram_a_all[...].reshape(HALF, HALF))
    first_copy = pltpu.make_async_copy(first, first_hbm, out_sem.at[2])
    first_copy.start()

    @pl.when(keeps_a)
    def _():
        landed(gram_z_a.at[pl.ds(0, NZ - 1)], has.at[0])
        landed(gram_in_a.at[pl.ds(1, 31)], kas.at[0])

    landed(gram_z_b.at[pl.ds(0, NZ - 1)], hbs.at[0])
    landed(gram_in_b.at[pl.ds(1, 31)], kbs.at[0])
    image_copy.wait()
    own_copy.wait()
    first_copy.wait()

    landed(gram_in_b.at[pl.ds(1, 31)], kbr.at[0])


def sums(embeddings, start_basis):
    rows = embeddings.shape[0]
    dma = lambda *n: pltpu.SemaphoreType.DMA(n)
    vmem = pltpu.VMEM
    return pl.pallas_call(
        gather_kernel,
        out_shape=(
            jax.ShapeDtypeStruct((rows, K), F32),
            jax.ShapeDtypeStruct((NC, PLANE, 8, 128), F32),
            jax.ShapeDtypeStruct((HALF, HALF), F32),
        ),
        in_specs=[pl.BlockSpec(memory_space=pl.ANY)] * 2,
        out_specs=(pl.BlockSpec(memory_space=pl.ANY),) * 3,
        scratch_shapes=[
            vmem((PARTS, rows, WIDE), F32),
            vmem((PARTS, rows, WIDE), BF16),
            vmem((PARTS, rows, WIDE), BF16),
            vmem((rows, K), F32),
            vmem((HALVES, PLANE, 8, OWN), F32),
            vmem((HALVES, PLANE, 8, OWN), F32),
            vmem((HALVES, PLANE, 8, OWN), F32),
            vmem((HALVES, PLANE - 1, 8, OWN), F32),
            vmem((HALVES, OWN_TILES, 8, 128), F32),
            vmem((NZ, 8, 128), F32),
            vmem((HALVES, PLANE, 8, D), F32),
            vmem((rows, K), F32),
            vmem((3, PLANE, 8, 128), F32),
            vmem((32, 8, 128), F32),
            vmem((32, 8, 128), F32),
            vmem((NZ, 8, 128), F32),
            vmem((NZ, 8, 128), F32),
            vmem((PLANE, 8, 128), F32),
            vmem((8, 128), F32),
            vmem((HALF, HALF), F32),
            dma(PARTS + 1),
            dma(HALVES), dma(HALVES),
            dma(HALVES), dma(HALVES),
            dma(HALVES, OWN_TILES), dma(1),
            dma(1), dma(HALVES, OWN_TILES),
            dma(HALVES), dma(HALVES, PLANE),
            dma(HALVES), dma(HALVES),
            dma(PLANE), dma(1),
            dma(1), dma(1),
            dma(1), dma(1),
            dma(1), dma(1),
            dma(1), dma(1),
            dma(1), dma(1),
            dma(3),
            pltpu.SemaphoreType.REGULAR,
        ],
        compiler_params=pltpu.CompilerParams(
            collective_id=0, has_side_effects=True, vmem_limit_bytes=VMEM_BYTES
        ),
        name="sums",
    )(embeddings, start_basis)


LEFT = (0, 0, 1, 0, 2, 1)
RIGHT = (0, 1, 0, 2, 0, 1)


def stacked(pieces, order):
    return jnp.concatenate([pieces[i] for i in order], 0)


def spread(block, size):
    return [jnp.broadcast_to(block[:, j:j + 1], (size, 128)) for j in range(size)]


def eliminate(panels):
    size = BLOCK
    rows = lax.broadcasted_iota(jnp.int32, (size, 128), 0)
    done = []
    strips = [panel[:size] for panel in panels]
    rest = [panel[size:] for panel in panels]
    for off in range(0, HALF, size):
        last = off + size == HALF
        cols = spread(strips[0][:, off:off + size], size)
        if not last:
            ahead = spread(strips[0][:, off + size:off + 2 * size].T, size)
            change = [0.0] * len(strips)
        scale = jnp.zeros((size, 128), F32)
        for j in range(0, size, 2):
            cj, cn = cols[j], cols[j + 1]
            a, b, d = cj[j:j + 1], cj[j + 1:j + 2], cn[j + 1:j + 2]
            q = 1.0 / (a * d - b * b)
            aq, bq, dq = a * q, b * q, d * q
            u = cj * dq - cn * bq
            v = cn * aq - cj * bq
            for k in range(j + 2, size):
                lo = (k // 8) * 8
                new = cols[k][lo:] - (u[lo:] * cj[k:k + 1] + v[lo:] * cn[k:k + 1])
                cols[k] = jnp.concatenate([cols[k][:lo], new], 0) if lo else new
            if not last:
                aj, an = ahead[j], ahead[j + 1]
                au = aj * dq - an * bq
                av = an * aq - aj * bq
                for k in range(j + 2, size):
                    ahead[k] = ahead[k] - (au * cj[k:k + 1] + av * cn[k:k + 1])
                change = [t + (au * s[j:j + 1] + av * s[j + 1:j + 2]) for t, s in zip(change, strips)]
            below = rows > j + 1
            ba = b * (1.0 / a)
            um = jnp.where(below, u, jnp.where(rows == j + 1, ba, 0.0))
            vm = jnp.where(below, v, 0.0)
            strips = [s - (um * s[j:j + 1] + vm * s[j + 1:j + 2]) for s in strips]
            ra = lax.rsqrt(a)
            rd = lax.rsqrt(d - ba * b)
            scale = jnp.where(rows == j, ra, jnp.where(rows == j + 1, rd, scale))
        strips = [s * scale for s in strips]
        done.append(strips[1:])
        if last:
            break
        following = [r[:size] - t for r, t in zip(rest, change)]
        behind = off + 2 * size
        if behind < HALF:
            pieces = [split3(s) for s in strips]
            left = stacked(pieces[0], LEFT)
            right = jnp.concatenate([stacked(piece, RIGHT) for piece in pieces], 1)
            product = mm(left, right, TN)[behind:]
            rest = [r[size:] - product[:, 128 * i:128 * (i + 1)] for i, r in enumerate(rest)]
        strips = following
    return [jnp.concatenate([strips[i] for strips in done], 0) for i in range(len(panels) - 1)]


def mm6(a, b, dims):
    ((left,), (right,)), _ = dims
    pa, pb = split3(a), split3(b)
    return mm(jnp.concatenate([pa[i] for i in LEFT], left), jnp.concatenate([pb[i] for i in RIGHT], right), dims)


def diagonal():
    return lax.broadcasted_iota(jnp.int32, (HALF, HALF), 0) == lax.broadcasted_iota(jnp.int32, (HALF, HALF), 1)


def diagonal_scales(value):
    entries = jnp.where(diagonal(), value, 0.0)
    return (
        lax.rsqrt(jnp.sum(entries, axis=1, keepdims=True)),
        lax.rsqrt(jnp.sum(entries, axis=0, keepdims=True)),
    )


def first_inverse(aa):
    col, row = diagonal_scales(aa)
    (inverse,) = eliminate([aa * col * row, jnp.where(diagonal(), 1.0, 0.0)])
    return inverse * row


def basis_kernel(scale, gram_hbm, first_hbm, image_hbm, out_hbm, gram, first_in, image, out, sems):
    loads = [
        pltpu.make_async_copy(src, dst, sems.at[i])
        for i, (src, dst) in enumerate([(gram_hbm, gram), (first_hbm, first_in), (image_hbm, image)])
    ]
    for copy in loads:
        copy.start()
    loads[0].wait()
    ba, bb = gram[0].reshape(HALF, HALF), gram[1].reshape(HALF, HALF)
    col, row = diagonal_scales(bb)
    loads[1].wait()
    first = first_in[...]
    cross = mm6(ba * col, first, NT)
    rest = bb * col * row - mm6(cross, cross, NT)
    lower = mm6(cross, first, NN)
    loads[2].wait()
    rows = image.shape[0]
    outs = []

    def product(value, factor):
        hi, lo = split2(value)
        high, low = split2(factor)
        both = mm(hi, jnp.concatenate([high, low], 0), NT)
        return both[:, :HALF] + (both[:, HALF:] + mm(lo, high, NT))

    def leave(r, n, cols):
        outs.append(pltpu.make_async_copy(out.at[pl.ds(r, n), cols], out_hbm.at[pl.ds(r, n), cols], sems.at[3 + len(outs)]))
        outs[-1].start()

    out[:, :HALF] = product(image[:, :HALF], first * scale)
    leave(0, rows, pl.ds(0, HALF))
    below, second = eliminate([rest, -lower, jnp.where(diagonal(), 1.0, 0.0)])
    factor = jnp.concatenate([below, second * row], 1) * scale
    step = rows // 4
    for r in range(0, rows, step):
        out[r:r + step, HALF:] = product(image[r:r + step, :], factor)
        leave(r, step, pl.ds(HALF, HALF))
    for copy in outs:
        copy.wait()


def basis_of(gram, first, image, scale):
    rows = image.shape[0]
    return pl.pallas_call(
        functools.partial(basis_kernel, scale),
        out_shape=jax.ShapeDtypeStruct((rows, K), F32),
        in_specs=[pl.BlockSpec(memory_space=pl.ANY)] * 3,
        out_specs=pl.BlockSpec(memory_space=pl.ANY),
        scratch_shapes=[
            pltpu.VMEM((NC, PLANE, 8, 128), F32),
            pltpu.VMEM((HALF, HALF), F32),
            pltpu.VMEM((rows, K), F32),
            pltpu.VMEM((rows, K), F32),
            pltpu.SemaphoreType.DMA((8,)),
        ],
        compiler_params=pltpu.CompilerParams(vmem_limit_bytes=VMEM_BYTES),
        name="basis",
    )(gram, first, image)


def local(embeddings, start_basis):
    total_rows = embeddings.shape[0] * lax.axis_size("dp")
    image, gram, first = sums(embeddings, start_basis)
    return basis_of(gram, first, image, float(total_rows) ** 0.5)


def solution(mesh):
    in_specs = (P("dp", None), P("dp", None))
    out_specs = P("dp", None)
    return jax.shard_map(local, mesh=mesh, in_specs=in_specs, out_specs=out_specs, check_vma=False)
```
